256 devices in a mesh: replica: 8 (over z), dp: 32 (over x, y, core).
Axes of the slice: x: 4, y: 4, z: 8, core: 2. Of those that a mesh axis runs over, the one named last changes fastest.
Arguments:
- activations: bfloat16 [196608, 4096], P(('replica', 'dp')), may hold values from -60 to 60
- cotangents: bfloat16 [196608, 1024], P(('replica', 'dp')), may hold values from -0.0390625 to 0.0390625
- error_buffer: float32 [32768, 1024], P(('replica', 'dp')), may hold values from -6 to 6
- master_weights: float32 [4096, 1024], P('dp'), may hold values from -0.75 to 0.75
- first_moment: float32 [4096, 1024], P('dp'), may hold values from -4 to 4
- second_moment: float32 [4096, 1024], P('dp'), may hold values from 0.05 to 2
- warm_factor: float32 [2, 64, 512], replicated, may hold values from -6 to 6
Outputs:
- new_weights: float32 [4096, 1024], P('dp')
- new_first: float32 [4096, 1024], P('dp')
- new_second: float32 [4096, 1024], P('dp')
- new_error: float32 [32768, 1024], P(('replica', 'dp'))
- new_factor: float32 [2, 64, 512], replicated
The draws below stay inside these ranges and needn't reach their ends.
All inputs are finite; a program needn't handle non-finite values.
Results may differ from the reference program's by a relative error of at most 0.0003.
Values may be sent and summed in bfloat16 or wider, within the bound.
A program may use at most 192 MiB of HBM per device.

```python
import math
import jax
import jax.numpy as jnp
from jax import lax

FEAT = 4096
KVCOLS = 512
RANK = 64
TOK_DEV = 768
REPLICAS = 8
BATCH = 196608
N_DP = 32


def draw_activations(key, part):
    key = jax.random.fold_in(key, 17)
    scale_key, base_key = jax.random.split(key, 2)
    feature_scale = jnp.exp(jax.random.uniform(scale_key, (1, FEAT), jnp.float32, -1.15, 1.15))
    values = jnp.clip(jax.random.normal(base_key, (BATCH, FEAT), jnp.float32), -5.0, 5.0) * feature_scale
    return values.astype(jnp.bfloat16)


def level_of(stream_key, dims, pieces, least, top_value):
    factor_of = 1.0
    for position, blocks in pieces:
        steps = jax.random.uniform(jax.random.fold_in(jax.random.fold_in(stream_key, 6), position), (blocks,), jnp.float32, least / len(pieces), top_value / len(pieces))
        factor_of = factor_of * jnp.repeat(jnp.exp(steps), dims[position] // blocks).reshape((-1,) + (1,) * (len(dims) - 1 - position))
    return factor_of


def scatter_about(own_key, dims, scale, most, cuts=(), kind=jnp.bfloat16):
    level = level_of(own_key, dims, cuts, -0.22, 0.18) if cuts else 1.0
    entries = jax.random.normal(own_key, dims, jnp.float32) * scale * level
    return jnp.minimum(jnp.maximum(entries, -most), most).astype(kind)


def setup_inputs(seed: int = 0) -> dict:
    seeds = jax.random.split(jax.random.key(seed), 8)
    return {
        "activations": draw_activations(jax.random.fold_in(seeds[7], 71), 0),
        "cotangents": scatter_about(seeds[1], (BATCH, 2 * KVCOLS), (TOK_DEV * N_DP) ** -0.5, 0.0390625, ((0, 256),)),
        "error_buffer": scatter_about(seeds[2], (REPLICAS * FEAT, 2 * KVCOLS), 1.0, 6.0, ((0, 256),), jnp.float32),
        "master_weights": scatter_about(seeds[3], (FEAT, 2 * KVCOLS), 0.05, 0.75, ((0, 32),), jnp.float32),
        "first_moment": scatter_about(seeds[4], (FEAT, 2 * KVCOLS), 0.3, 4.0, ((0, 32),), jnp.float32),
        "second_moment": jnp.clip(jnp.exp(math.log(2.0) - 3.6888794 * jax.random.uniform(seeds[5], (FEAT, 2 * KVCOLS), jnp.float32) ** level_of(seeds[5], (FEAT, 2 * KVCOLS), ((0, 32),), -0.2, 0.2)), 0.05, 2.0),
        "warm_factor": scatter_about(seeds[6], (2, RANK, KVCOLS), 1.0, 6.0, (), jnp.float32),
    }


highest = lax.Precision.HIGHEST
first_decay = 0.9
second_decay = 0.999
learn_rate = 0.01
adam_epsilon = 1e-08
step_count = 10

def adam_update(update, master_weights, first_moment, second_moment):
    new_first = first_decay * first_moment + (1.0 - first_decay) * update
    new_second = second_decay * second_moment + (1.0 - second_decay) * update * update
    first_hat = new_first / (1.0 - first_decay ** step_count)
    second_hat = new_second / (1.0 - second_decay ** step_count)
    new_weights = master_weights - learn_rate * first_hat / (jnp.sqrt(second_hat) + adam_epsilon)
    return (new_weights, new_first, new_second)

def orthonormal(columns):
    ortho_basis = jnp.zeros_like(columns)
    for column_index in range(RANK):
        column = columns[:, column_index]
        for sweep_index in range(2):
            coeffs = jnp.dot(column, ortho_basis, precision=highest)
            column = column - jnp.dot(ortho_basis, coeffs, precision=highest)
        ortho_basis = ortho_basis.at[:, column_index].set(column / jnp.sqrt(jnp.sum(column * column)))
    return ortho_basis

def add_block(running, members):
    acts_one, cots_one = members
    partial_sum = jnp.dot(acts_one.T, cots_one, preferred_element_type=jnp.float32)
    return (running + partial_sum, None)

def pod_gradient(members):
    start_sum = jnp.zeros((FEAT, 2 * KVCOLS), jnp.float32)
    running, unused = lax.scan(add_block, start_sum, members)
    return running

def reference(activations, cotangents, error_buffer, master_weights, first_moment, second_moment, warm_factor):
    grouped_acts = activations.reshape(REPLICAS, N_DP, TOK_DEV, FEAT)
    grouped_cots = cotangents.reshape(REPLICAS, N_DP, TOK_DEV, 2 * KVCOLS)
    pod_grad = lax.map(pod_gradient, (grouped_acts, grouped_cots))
    corrected = pod_grad + error_buffer.reshape(REPLICAS, FEAT, 2 * KVCOLS)
    split_cols = corrected.reshape(REPLICAS, FEAT, 2, KVCOLS)
    approx_parts = []
    factors = []
    for matrix_index in range(2):
        matrix_block = split_cols[:, :, matrix_index, :]
        power_sum = jnp.einsum('rfc,kc->fk', matrix_block, warm_factor[matrix_index], precision=highest)
        ortho_basis = orthonormal(power_sum)
        factor_mean = jnp.einsum('rfc,fk->kc', matrix_block, ortho_basis, precision=highest) / REPLICAS
        approx_parts.append(jnp.dot(ortho_basis, factor_mean, precision=highest))
        factors.append(factor_mean)
    approx = jnp.stack(approx_parts, axis=1).reshape(FEAT, 2 * KVCOLS)
    new_error = (corrected - approx[None]).reshape(REPLICAS * FEAT, 2 * KVCOLS)
    new_weights, new_first, new_second = adam_update(approx, master_weights, first_moment, second_moment)
    return (new_weights, new_first, new_second, new_error, jnp.stack(factors))
```

```python
import jax
import jax.numpy as jnp
from jax import lax
from jax.experimental import pallas as pl
from jax.experimental.pallas import tpu as pltpu
from jax.sharding import PartitionSpec as P

highest = lax.Precision.HIGHEST
first_decay = 0.9
second_decay = 0.999
learn_rate = 0.01
adam_epsilon = 1e-08
step_count = 10

F32 = jnp.float32
BF16 = jnp.bfloat16
RING = 4
DEPTH = 8
OFFSETS = (2, 1, 3, 0)


def dot_t(a, b):
    return lax.dot_general(a, b, (((1,), (1,)), ((), ())), precision=highest, preferred_element_type=F32)


def dot_n(a, b):
    return jnp.dot(a, b, precision=highest, preferred_element_type=F32)


class Wire:
    def __init__(self, send, recv):
        self.send, self.recv, self.copies = send, recv, []

    def start(self, src, dst, device):
        i = len(self.copies)
        copy = pltpu.make_async_remote_copy(
            src_ref=src, dst_ref=dst, send_sem=self.send.at[i], recv_sem=self.recv.at[i],
            device_id=device, device_id_type=pl.DeviceIdType.MESH,
        )
        copy.start()
        self.copies.append(copy)
        return copy

    def drain(self):
        for copy in self.copies:
            copy.wait_send()


class Local:
    def __init__(self, sems):
        self.sems, self.count = sems, 0

    def start(self, src, dst):
        copy = pltpu.make_async_copy(src, dst, self.sems.at[self.count])
        copy.start()
        self.count += 1
        return copy


def kernel_a(
    acts, cots, err, warm,
    corr_out, pt_out, linv_out, n_out,
    acts_v, cots_v, cots_t, own, rel_a, rel_b, from_m, from_p, rel2_a, rel2_b, from2_m, from2_p,
    err_v, warm_v, m_t, pt_loc, zr, zsum, n_loc, n_rx, g_loc, g_rx, ns, ra, na, rb, nb, zs, nz, na2, ga, gb, g_half, g_all,
    t_mat, send_sem, recv_sem, loc_sem,
):
    z = lax.axis_index("replica")
    dp = lax.axis_index("dp")
    c = dp % 2
    x = dp // 8
    y = (dp // 2) % 4
    p = x * (1 - c) + y * c
    q = y * (1 - c) + x * c
    sa = 8 - 6 * c
    sb = 2 + 6 * c
    tokens = cots.shape[0]

    def at(pp, qq):
        return (z, (pp % 4) * sa + (qq % 4) * sb + c)

    def along_a(k):
        return at(p + k, q)

    def along_b(k):
        return at(p, q + k)

    def along_z(k):
        return ((z + k) % DEPTH, dp)

    partner = (z, dp + 1 - 2 * c)

    def own_cols(t, s):
        d = ((p + OFFSETS[s]) % 4) * sa + ((q + OFFSETS[t]) % 4) * sb + c
        return pl.ds(pl.multiple_of(d * 128, 128), 128)

    def partner_cols(t, s):
        d = ((q + OFFSETS[s]) % 4) * sb + ((p + OFFSETS[t]) % 4) * sa + 1 - c
        return pl.ds(pl.multiple_of(d * 128, 128), 128)

    wire = Wire(send_sem, recv_sem)
    local = Local(loc_sem)

    cots_here = local.start(cots, cots_v.at[0])
    acts_here = [[None] * 4 for _ in range(4)]
    acts_there = [[None] * 4 for _ in range(4)]
    for s in range(4):
        acts_here[0][s] = local.start(acts.at[:, own_cols(0, s)], acts_v.at[0, pl.ds(0, tokens), pl.ds(128 * s, 128)])

    barrier = pltpu.get_barrier_semaphore()
    friends = [partner] + [along_a(k) for k in (1, 2, 3)] + [along_b(k) for k in (1, 2, 3)] + [along_z(k) for k in range(1, DEPTH)]
    for friend in friends:
        pl.semaphore_signal(barrier, inc=1, device_id=friend, device_id_type=pl.DeviceIdType.MESH)
    pl.semaphore_wait(barrier, len(friends))

    cots_there = wire.start(cots, cots_v.at[1], partner)
    for t in range(4):
        for s in range(4):
            if t > 0:
                acts_here[t][s] = local.start(
                    acts.at[:, own_cols(t, s)], acts_v.at[t, pl.ds(0, tokens), pl.ds(128 * s, 128)])
            acts_there[t][s] = wire.start(
                acts.at[:, partner_cols(t, s)], acts_v.at[t, pl.ds(tokens, tokens), pl.ds(128 * s, 128)], partner)
    err_copy = local.start(err, err_v)
    warm_copy = local.start(warm, warm_v)

    def turn(h):
        @pl.loop(0, 8)
        def _(i):
            cols = pl.ds(pl.multiple_of(i * 128, 128), 128)
            cots_t[cols, h * tokens:(h + 1) * tokens] = cots_v[h, :, cols].T

    cots_here.wait()
    turn(0)
    cots_there.wait_recv()
    turn(1)

    def compute(t):
        for s in range(4):
            acts_here[t][s].wait()
            acts_there[t][s].wait_recv()

        @pl.loop(0, 4)
        def _(i):
            rows = pl.ds(pl.multiple_of(i * 256, 256), 256)
            part = jnp.dot(cots_t[rows, :], acts_v[t], preferred_element_type=F32)
            for s in range(4):
                own[t, s, rows, :] = part[:, 128 * s:128 * (s + 1)]

    lo, hi = pl.ds(0, 512), pl.ds(512, 512)
    relay_a, relay_b, outer_m, outer_p, inner_m, inner_p = ([None] * 4 for _ in range(6))

    def send_relay(t):
        relay_a[t] = wire.start(own.at[t, 0, lo], rel_a.at[t], along_a(1))
        relay_b[t] = wire.start(own.at[t, 0, hi], rel_b.at[t], along_a(3))

    def send_outer(t):
        outer_m[t] = wire.start(own.at[t, 1, hi], from_m.at[t, hi], along_a(1))
        outer_p[t] = wire.start(own.at[t, 2, lo], from_p.at[t, lo], along_a(3))

    def send_inner(t):
        relay_a[t].wait_recv()
        own[t, 1, lo, :] += rel_a[t]
        inner_m[t] = wire.start(own.at[t, 1, lo], from_m.at[t, lo], along_a(1))
        relay_b[t].wait_recv()
        own[t, 2, hi, :] += rel_b[t]
        inner_p[t] = wire.start(own.at[t, 2, hi], from_p.at[t, hi], along_a(3))

    def gather(t):
        for copy in (outer_m[t], outer_p[t], inner_m[t], inner_p[t]):
            copy.wait_recv()
        own[t, 3] += from_m[t] + from_p[t]

    compute(0)
    send_relay(0)
    send_outer(0)
    compute(1)
    send_relay(1)
    send_inner(0)
    send_outer(1)
    compute(2)
    send_relay(2)
    send_inner(1)
    send_outer(2)
    gather(0)
    second_a = wire.start(own.at[0, 3, lo], rel2_a, along_b(1))
    second_b = wire.start(own.at[0, 3, hi], rel2_b, along_b(3))
    compute(3)
    send_relay(3)
    send_inner(2)
    send_outer(3)
    gather(1)
    outer2_m = wire.start(own.at[1, 3, hi], from2_m.at[hi], along_b(1))
    second_a.wait_recv()
    own[1, 3, lo, :] += rel2_a[...]
    inner2_m = wire.start(own.at[1, 3, lo], from2_m.at[lo], along_b(1))
    send_inner(3)
    gather(2)
    outer2_p = wire.start(own.at[2, 3, lo], from2_p.at[lo], along_b(3))
    second_b.wait_recv()
    own[2, 3, hi, :] += rel2_b[...]
    inner2_p = wire.start(own.at[2, 3, hi], from2_p.at[hi], along_b(3))

    err_copy.wait()
    for i in range(8):
        m_t[128 * i:128 * (i + 1), :] = err_v[:, 128 * i:128 * (i + 1)].T
    gather(3)
    for copy in (outer2_m, inner2_m, outer2_p, inner2_p):
        copy.wait_recv()
    m_t[...] += own[3, 3] + (from2_m[...] + from2_p[...])

    warm_copy.wait()
    for j in range(2):
        pt_loc[64 * j:64 * (j + 1), :] = dot_n(warm_v[j], m_t[512 * j:512 * (j + 1), :])

    def z_rows(zz):
        return pl.ds(pl.multiple_of((zz % DEPTH) * 16, 16), 16)

    scatter = [wire.start(pt_loc.at[z_rows(z + k)], zr.at[k], along_z(k)) for k in range(1, DEPTH)]
    total = pt_loc[z_rows(z), :]
    for k in range(1, DEPTH):
        scatter[k - 1].wait_recv()
        total = total + zr[k]
    zsum[...] = total
    spread = [wire.start(zsum, pt_out.at[z_rows(z)], along_z(k)) for k in range(1, DEPTH)]
    pt_out[z_rows(z), :] = total
    for i in range(8):
        corr_out[:, 128 * i:128 * (i + 1)] = m_t[128 * i:128 * (i + 1), :].T
    for copy in spread:
        copy.wait_recv()

    pt = pt_out[...]
    lane = lax.broadcasted_iota(jnp.int32, (64, 128), 1)
    gram = dot_t(pt, pt)
    g_loc[...] = jnp.where(lane < 64, gram[0:64], gram[64:128])
    g_swap = wire.start(g_loc, g_rx, partner)
    for j in range(2):
        for i in range(4):
            n_loc[j, 64 * i:64 * (i + 1), :] = dot_t(
                pt[64 * j:64 * (j + 1)], m_t[512 * j + 128 * i:512 * j + 128 * (i + 1), :])
    n_swap = wire.start(n_loc.at[1 - c], n_rx, partner)

    half = pl.ds(pl.multiple_of(c * 32, 32), 32)
    g_swap.wait_recv()
    ga[p] = g_loc[half, :] + g_rx[half, :]
    ga_copies = [wire.start(ga.at[p], ga.at[p], along_a(k)) for k in (1, 2, 3)]

    n_swap.wait_recv()
    ns[...] = n_loc[c] + n_rx[...]

    def rows_of(index, size):
        return pl.ds(pl.multiple_of((index % 4) * size, size), size)

    ra_copies = [wire.start(ns.at[rows_of(p + k, 64)], ra.at[k], along_a(k)) for k in (1, 2, 3)]
    for copy in ga_copies:
        copy.wait_recv()
    gb[q] = (ga[0] + ga[1]) + (ga[2] + ga[3])
    gb_copies = [wire.start(gb.at[q], gb.at[q], along_b(k)) for k in (1, 2, 3)]
    for copy in ra_copies:
        copy.wait_recv()
    na[...] = (ns[rows_of(p, 64), :] + ra[1]) + (ra[2] + ra[3])
    rb_copies = [wire.start(na.at[rows_of(q + k, 16)], rb.at[k], along_b(k)) for k in (1, 2, 3)]
    for copy in gb_copies:
        copy.wait_recv()
    g_part = (gb[0] + gb[1]) + (gb[2] + gb[3])
    g_half[...] = g_part
    g_all[half, :] = g_part
    g_back = wire.start(g_half, g_all.at[half], partner)
    for copy in rb_copies:
        copy.wait_recv()
    nb[...] = (na[rows_of(q, 16), :] + rb[1]) + (rb[2] + rb[3])
    zs_copies = [wire.start(nb, zs.at[z], along_z(k)) for k in range(1, DEPTH)]
    zs[z] = nb[...]

    g_back.wait_recv()
    row = lax.broadcasted_iota(jnp.int32, (64, 128), 0)
    g = g_all[...]
    eye = jnp.where(lane == row, 1.0, 0.0).astype(F32)
    t_mat[0] = jnp.where(lane >= 64, pltpu.roll(g, 64, 1), eye)
    t_mat[1] = jnp.where(lane >= 64, g, eye)

    def eliminate(first, last):
        for k in range(first, last):
            base = 8 * (k // 8)
            below = lax.broadcasted_iota(jnp.int32, (64 - base, 1), 0) > k - base
            for j in range(2):
                pivot_row = t_mat[j, k:k + 1, :]
                inv = 1.0 / jnp.sqrt(pivot_row[:, 64 + k:65 + k])
                scaled = pivot_row * inv
                column = t_mat[j, base:64, 64 + k:65 + k] * inv
                column = jnp.where(below, column, 0.0)
                t_mat[j, base:64, :] -= column * scaled
                t_mat[j, k:k + 1, :] = scaled

    eliminate(0, 20)
    for copy in zs_copies:
        copy.wait_recv()
    nz[...] = ((zs[0] + zs[1]) + (zs[2] + zs[3])) + ((zs[4] + zs[5]) + (zs[6] + zs[7]))
    back_b = [wire.start(nz, na2.at[rows_of(q, 16)], along_b(k)) for k in (1, 2, 3)]
    na2[rows_of(q, 16), :] = nz[...]
    eliminate(20, 35)
    for copy in back_b:
        copy.wait_recv()
    back_a = [wire.start(na2, n_out.at[c, rows_of(p, 64)], along_a(k)) for k in (1, 2, 3)]
    n_out[c, rows_of(p, 64), :] = na2[...]
    eliminate(35, 50)
    for copy in back_a:
        copy.wait_recv()
    back_c = wire.start(n_out.at[c], n_out.at[c], partner)
    eliminate(50, 64)
    linv_out[...] = t_mat[...]
    back_c.wait_recv()
    wire.drain()


def kernel_b(corr, pt, linv, n, weights, first, second, w_out, first_out, second_out, err_out, factor_out):
    for j in range(2):
        inverse = linv[j][:, 0:64]
        basis = dot_n(inverse, pt[64 * j:64 * (j + 1), :]).T
        for i in range(4):
            cols = slice(512 * j + 128 * i, 512 * j + 128 * (i + 1))
            factor = dot_n(inverse, n[j, 64 * i:64 * (i + 1), :]) * 0.125
            factor_out[j, :, 128 * i:128 * (i + 1)] = factor
            approx = dot_n(basis, factor)
            err_out[:, cols] = corr[:, cols] - approx
            new_first = first_decay * first[:, cols] + (1.0 - first_decay) * approx
            new_second = second_decay * second[:, cols] + (1.0 - second_decay) * approx * approx
            first_out[:, cols] = new_first
            second_out[:, cols] = new_second
            first_hat = new_first / (1.0 - first_decay**step_count)
            second_hat = new_second / (1.0 - second_decay**step_count)
            w_out[:, cols] = weights[:, cols] - learn_rate * first_hat / (jnp.sqrt(second_hat) + adam_epsilon)


def local(activations, cotangents, error_buffer, master_weights, first_moment, second_moment, warm_factor):
    tokens = activations.shape[0]
    rows, cols = error_buffer.shape
    shape = jax.ShapeDtypeStruct
    vmem = pl.BlockSpec(memory_space=pltpu.VMEM)
    anywhere = pl.BlockSpec(memory_space=pl.ANY)
    copies = 120
    corr, pt, linv, n = pl.pallas_call(
        kernel_a,
        out_shape=(shape((rows, cols), F32), shape((128, 128), F32), shape((2, 64, 128), F32), shape((2, 256, 128), F32)),
        in_specs=[anywhere] * 4,
        out_specs=(vmem,) * 4,
        scratch_shapes=[
            pltpu.VMEM((4, 2 * tokens, 512), BF16),
            pltpu.VMEM((2, tokens, cols), BF16),
            pltpu.VMEM((cols, 2 * tokens), BF16),
            pltpu.VMEM((4, 4, cols, 128), F32),
            pltpu.VMEM((4, 512, 128), F32),
            pltpu.VMEM((4, 512, 128), F32),
            pltpu.VMEM((4, cols, 128), F32),
            pltpu.VMEM((4, cols, 128), F32),
            pltpu.VMEM((512, 128), F32),
            pltpu.VMEM((512, 128), F32),
            pltpu.VMEM((cols, 128), F32),
            pltpu.VMEM((cols, 128), F32),
            pltpu.VMEM((rows, cols), F32),
            pltpu.VMEM((2, 64, 512), F32),
            pltpu.VMEM((cols, 128), F32),
            pltpu.VMEM((128, 128), F32),
            pltpu.VMEM((8, 16, 128), F32),
            pltpu.VMEM((16, 128), F32),
            pltpu.VMEM((2, 256, 128), F32),
            pltpu.VMEM((256, 128), F32),
            pltpu.VMEM((64, 128), F32),
            pltpu.VMEM((64, 128), F32),
            pltpu.VMEM((256, 128), F32),
            pltpu.VMEM((4, 64, 128), F32),
            pltpu.VMEM((64, 128), F32),
            pltpu.VMEM((4, 16, 128), F32),
            pltpu.VMEM((16, 128), F32),
            pltpu.VMEM((8, 16, 128), F32),
            pltpu.VMEM((16, 128), F32),
            pltpu.VMEM((64, 128), F32),
            pltpu.VMEM((4, 32, 128), F32),
            pltpu.VMEM((4, 32, 128), F32),
            pltpu.VMEM((32, 128), F32),
            pltpu.VMEM((64, 128), F32),
            pltpu.VMEM((2, 64, 128), F32),
            pltpu.SemaphoreType.DMA((copies,)),
            pltpu.SemaphoreType.DMA((copies,)),
            pltpu.SemaphoreType.DMA((24,)),
        ],
        compiler_params=pltpu.CompilerParams(
            collective_id=0, has_side_effects=True, vmem_limit_bytes=44 * 1024 * 1024),
    )(activations, cotangents, error_buffer, warm_factor)
    tile = shape((rows, cols), F32)
    return pl.pallas_call(
        kernel_b,
        out_shape=(tile, tile, tile, tile, shape(warm_factor.shape, F32)),
        in_specs=[vmem] * 7,
        out_specs=(vmem,) * 5,
        compiler_params=pltpu.CompilerParams(vmem_limit_bytes=16 * 1024 * 1024),
    )(corr, pt, linv, n, master_weights, first_moment, second_moment)


def solution(mesh):
    placed = (
        P(("replica", "dp"), None),
        P(("replica", "dp"), None),
        P(("replica", "dp"), None),
        P("dp", None),
        P("dp", None),
        P("dp", None),
        P(),
    )
    return jax.shard_map(
        local,
        mesh=mesh,
        in_specs=placed,
        out_specs=(P("dp", None), P("dp", None), P("dp", None), P(("replica", "dp"), None), P()),
        check_vma=False,
    )
```

```python
import jax
import jax.numpy as jnp
from jax import lax
from jax.experimental import pallas as pl
from jax.experimental.pallas import tpu as pltpu
from jax.sharding import PartitionSpec as P

highest = lax.Precision.HIGHEST
first_decay = 0.9
second_decay = 0.999
learn_rate = 0.01
adam_epsilon = 1e-08
step_count = 10

F32 = jnp.float32
BF16 = jnp.bfloat16
DEPTH = 8
SPAN = 174.0
OFFSETS = (2, 1, 3, 0)


def dot_t(a, b):
    return lax.dot_general(a, b, (((1,), (1,)), ((), ())), precision=highest, preferred_element_type=F32)


def dot_n(a, b):
    return jnp.dot(a, b, precision=highest, preferred_element_type=F32)


def encode(source, code):
    tiles = [slice(128 * i, 128 * (i + 1)) for i in range(4)]
    top = jnp.abs(source[tiles[0], :])
    for tile in tiles[1:]:
        top = jnp.maximum(top, jnp.abs(source[tile, :]))
    top = jnp.maximum(jnp.max(top, axis=0, keepdims=True) * 1.004, 1e-30).astype(BF16)
    code[512:528, :] = jnp.broadcast_to(top, (16, 128))
    scale = SPAN / top.astype(F32)
    for tile in tiles:
        value = source[tile, :]
        size = jnp.exp(jnp.abs(value) * scale - 0.5 * SPAN)
        code[tile, :] = jnp.where(value < 0.0, -size, size).astype(BF16)


def decode(code, tile):
    scale = code[512:528, :].astype(F32)[0:1] * (1.0 / SPAN)
    value = code[tile, :].astype(F32)
    size = (jnp.log(jnp.abs(value)) + 0.5 * SPAN) * scale
    return jnp.where(value < 0.0, -size, size)


class Wire:
    def __init__(self, send, recv):
        self.send, self.recv, self.copies = send, recv, []

    def start(self, src, dst, device):
        i = len(self.copies)
        copy = pltpu.make_async_remote_copy(
            src_ref=src, dst_ref=dst, send_sem=self.send.at[i], recv_sem=self.recv.at[i],
            device_id=device, device_id_type=pl.DeviceIdType.MESH,
        )
        copy.start()
        self.copies.append(copy)
        return copy

    def drain(self):
        for copy in self.copies:
            copy.wait_send()


class Local:
    def __init__(self, sems):
        self.sems, self.count = sems, 0

    def start(self, src, dst):
        copy = pltpu.make_async_copy(src, dst, self.sems.at[self.count])
        copy.start()
        self.count += 1
        return copy


def kernel_a(
    acts, cots, err, warm,
    corr_out, pt_out, linv_out, n_out,
    acts_v, cots_v, cots_t, own, tx, rx,
    err_v, warm_v, pt_loc, zr, zsum, n_loc, n_rx, g_loc, g_rx, ns, ra, nb, zs, nz, ga, gb, g_half, g_all,
    t_mat, send_sem, recv_sem, loc_sem,
):
    z = lax.axis_index("replica")
    dp = lax.axis_index("dp")
    c = dp % 2
    x = dp // 8
    y = (dp // 2) % 4
    p = x * (1 - c) + y * c
    q = y * (1 - c) + x * c
    sa = 8 - 6 * c
    sb = 2 + 6 * c
    tokens = cots.shape[0]

    def at(pp, qq):
        return (z, (pp % 4) * sa + (qq % 4) * sb + c)

    def along_a(k):
        return at(p + k, q)

    def along_b(k):
        return at(p, q + k)

    def along_z(k):
        return ((z + k) % DEPTH, dp)

    partner = (z, dp + 1 - 2 * c)

    def own_cols(t, s):
        d = ((p + OFFSETS[s]) % 4) * sa + ((q + OFFSETS[t]) % 4) * sb + c
        return pl.ds(pl.multiple_of(d * 128, 128), 128)

    def partner_cols(t, s):
        d = ((q + OFFSETS[s]) % 4) * sb + ((p + OFFSETS[t]) % 4) * sa + 1 - c
        return pl.ds(pl.multiple_of(d * 128, 128), 128)

    wire = Wire(send_sem, recv_sem)
    local = Local(loc_sem)

    cots_here = local.start(cots, cots_v.at[0])
    acts_here = [[None] * 4 for _ in range(4)]
    acts_there = [[None] * 4 for _ in range(4)]
    for s in range(4):
        acts_here[0][s] = local.start(acts.at[:, own_cols(0, s)], acts_v.at[0, pl.ds(0, tokens), pl.ds(128 * s, 128)])

    barrier = pltpu.get_barrier_semaphore()
    friends = [partner] + [at(p + i, q + j) for i in range(4) for j in range(4) if i or j] + [along_z(k) for k in range(1, DEPTH)]
    for friend in friends:
        pl.semaphore_signal(barrier, inc=1, device_id=friend, device_id_type=pl.DeviceIdType.MESH)
    pl.semaphore_wait(barrier, len(friends))

    cots_there = wire.start(cots, cots_v.at[1], partner)
    for t in range(4):
        for s in range(4):
            if t > 0:
                acts_here[t][s] = local.start(
                    acts.at[:, own_cols(t, s)], acts_v.at[t, pl.ds(0, tokens), pl.ds(128 * s, 128)])
            acts_there[t][s] = wire.start(
                acts.at[:, partner_cols(t, s)], acts_v.at[t, pl.ds(tokens, tokens), pl.ds(128 * s, 128)], partner)
    err_copy = local.start(err, err_v)
    warm_copy = local.start(warm, warm_v)

    def turn(h):
        @pl.loop(0, 8)
        def _(i):
            cols = pl.ds(pl.multiple_of(i * 128, 128), 128)
            cots_t[cols, h * tokens:(h + 1) * tokens] = cots_v[h, :, cols].T

    cots_here.wait()
    turn(0)
    cots_there.wait_recv()
    turn(1)

    def compute(t):
        for s in range(4):
            acts_here[t][s].wait()
            acts_there[t][s].wait_recv()

        @pl.loop(0, 4)
        def _(i):
            rows = pl.ds(pl.multiple_of(i * 256, 256), 256)
            part = jnp.dot(cots_t[rows, :], acts_v[t], preferred_element_type=F32)
            for s in range(4):
                own[t, s, rows, :] = part[:, 128 * s:128 * (s + 1)]

    slots = []

    def ship(source, device):
        i = len(slots)
        encode(source, tx.at[i])
        slots.append(wire.start(tx.at[i], rx.at[i], device))
        return i

    def absorb(target, *arrived):
        for i in arrived:
            slots[i].wait_recv()
        for i in range(4):
            tile = slice(128 * i, 128 * (i + 1))
            total = target[tile, :]
            for slot in arrived:
                total = total + decode(rx.at[slot], tile)
            target[tile, :] = total

    lo, hi = pl.ds(0, 512), pl.ds(512, 512)
    relay_a, relay_b, outer_m, outer_p, inner_m, inner_p = ([None] * 4 for _ in range(6))

    def send_relay(t):
        relay_a[t] = ship(own.at[t, 0, lo], along_a(1))
        relay_b[t] = ship(own.at[t, 0, hi], along_a(3))

    def send_outer(t):
        outer_m[t] = ship(own.at[t, 1, hi], along_a(1))
        outer_p[t] = ship(own.at[t, 2, lo], along_a(3))

    def send_inner(t):
        absorb(own.at[t, 1, lo], relay_a[t])
        inner_m[t] = ship(own.at[t, 1, lo], along_a(1))
        absorb(own.at[t, 2, hi], relay_b[t])
        inner_p[t] = ship(own.at[t, 2, hi], along_a(3))

    def gather(t):
        absorb(own.at[t, 3, lo], outer_p[t], inner_m[t])
        absorb(own.at[t, 3, hi], outer_m[t], inner_p[t])

    compute(0)
    send_relay(0)
    send_outer(0)
    compute(1)
    send_relay(1)
    send_inner(0)
    send_outer(1)
    compute(2)
    send_relay(2)
    send_inner(1)
    send_outer(2)
    gather(0)
    second_a = ship(own.at[0, 3, lo], along_b(1))
    second_b = ship(own.at[0, 3, hi], along_b(3))
    compute(3)
    send_relay(3)
    send_inner(2)
    send_outer(3)
    gather(1)
    outer2_m = ship(own.at[1, 3, hi], along_b(1))
    absorb(own.at[1, 3, lo], second_a)
    inner2_m = ship(own.at[1, 3, lo], along_b(1))
    send_inner(3)
    gather(2)
    outer2_p = ship(own.at[2, 3, lo], along_b(3))
    absorb(own.at[2, 3, hi], second_b)
    inner2_p = ship(own.at[2, 3, hi], along_b(3))

    err_copy.wait()
    for i in range(8):
        own[3, 3, 128 * i:128 * (i + 1), :] += err_v[:, 128 * i:128 * (i + 1)].T
    m_t = own.at[3, 3]
    absorb(own.at[3, 3, lo], outer_p[3], inner_m[3], outer2_p, inner2_m)
    absorb(own.at[3, 3, hi], outer_m[3], inner_p[3], outer2_m, inner2_p)

    warm_copy.wait()
    for j in range(2):
        pt_loc[64 * j:64 * (j + 1), :] = dot_n(warm_v[j], m_t[512 * j:512 * (j + 1), :])

    def z_rows(zz):
        return pl.ds(pl.multiple_of((zz % DEPTH) * 16, 16), 16)

    scatter = [wire.start(pt_loc.at[z_rows(z + k)], zr.at[k], along_z(k)) for k in range(1, DEPTH)]
    total = pt_loc[z_rows(z), :]
    for k in range(1, DEPTH):
        scatter[k - 1].wait_recv()
        total = total + zr[k]
    zsum[...] = total
    spread = [wire.start(zsum, pt_out.at[z_rows(z)], along_z(k)) for k in range(1, DEPTH)]
    pt_out[z_rows(z), :] = total
    for i in range(8):
        corr_out[:, 128 * i:128 * (i + 1)] = m_t[128 * i:128 * (i + 1), :].T
    for copy in spread:
        copy.wait_recv()

    pt = pt_out[...]
    lane = lax.broadcasted_iota(jnp.int32, (64, 128), 1)
    gram = dot_t(pt, pt)
    g_loc[...] = jnp.where(lane < 64, gram[0:64], gram[64:128])
    g_swap = wire.start(g_loc, g_rx, partner)
    for j in range(2):
        for i in range(4):
            n_loc[j, 64 * i:64 * (i + 1), :] = dot_t(
                pt[64 * j:64 * (j + 1)], m_t[512 * j + 128 * i:512 * j + 128 * (i + 1), :])
    n_swap = wire.start(n_loc.at[1 - c], n_rx, partner)

    half = pl.ds(pl.multiple_of(c * 32, 32), 32)
    g_swap.wait_recv()
    ga[p] = g_loc[half, :] + g_rx[half, :]
    ga_copies = [wire.start(ga.at[p], ga.at[p], along_a(k)) for k in (1, 2, 3)]

    n_swap.wait_recv()
    ns[...] = n_loc[c] + n_rx[...]

    def block(i, j):
        return pl.ds(pl.multiple_of((((p + i) % 4) * 4 + (q + j) % 4) * 16, 16), 16)

    others = [(i, j) for i in range(4) for j in range(4) if i or j]
    ra_copies = [wire.start(ns.at[block(i, j)], ra.at[4 * i + j], at(p + i, q + j)) for i, j in others]
    for copy in ga_copies:
        copy.wait_recv()
    gb[q] = (ga[0] + ga[1]) + (ga[2] + ga[3])
    gb_copies = [wire.start(gb.at[q], gb.at[q], along_b(k)) for k in (1, 2, 3)]
    for copy in gb_copies:
        copy.wait_recv()
    g_part = (gb[0] + gb[1]) + (gb[2] + gb[3])
    g_half[...] = g_part
    g_all[half, :] = g_part
    g_back = wire.start(g_half, g_all.at[half], partner)
    for copy in ra_copies:
        copy.wait_recv()
    total = ns[block(0, 0), :]
    for i, j in others:
        total = total + ra[4 * i + j]
    nb[...] = total
    zs_copies = [wire.start(nb, zs.at[z], along_z(k)) for k in range(1, DEPTH)]
    zs[z] = nb[...]

    g_back.wait_recv()
    row = lax.broadcasted_iota(jnp.int32, (64, 128), 0)
    g = g_all[...]
    eye = jnp.where(lane == row, 1.0, 0.0).astype(F32)
    t_mat[0] = jnp.where(lane >= 64, pltpu.roll(g, 64, 1), eye)
    t_mat[1] = jnp.where(lane >= 64, g, eye)

    def eliminate(first, last):
        for k in range(first, last):
            base = 8 * (k // 8)
            below = lax.broadcasted_iota(jnp.int32, (64 - base, 1), 0) > k - base
            for j in range(2):
                pivot_row = t_mat[j, k:k + 1, :]
                inv = 1.0 / jnp.sqrt(pivot_row[:, 64 + k:65 + k])
                scaled = pivot_row * inv
                column = t_mat[j, base:64, 64 + k:65 + k] * inv
                column = jnp.where(below, column, 0.0)
                t_mat[j, base:64, :] -= column * scaled
                t_mat[j, k:k + 1, :] = scaled

    eliminate(0, 20)
    for copy in zs_copies:
        copy.wait_recv()
    nz[...] = ((zs[0] + zs[1]) + (zs[2] + zs[3])) + ((zs[4] + zs[5]) + (zs[6] + zs[7]))
    back = [wire.start(nz, n_out.at[c, block(0, 0)], at(p + i, q + j)) for i, j in others]
    n_out[c, block(0, 0), :] = nz[...]
    eliminate(20, 50)
    for copy in back:
        copy.wait_recv()
    back_c = wire.start(n_out.at[c], n_out.at[c], partner)
    eliminate(50, 64)
    linv_out[...] = t_mat[...]
    back_c.wait_recv()
    wire.drain()


def kernel_b(corr, pt, linv, n, weights, first, second, w_out, first_out, second_out, err_out, factor_out):
    for j in range(2):
        inverse = linv[j][:, 0:64]
        basis = dot_n(inverse, pt[64 * j:64 * (j + 1), :]).T
        for i in range(4):
            cols = slice(512 * j + 128 * i, 512 * j + 128 * (i + 1))
            factor = dot_n(inverse, n[j, 64 * i:64 * (i + 1), :]) * 0.125
            factor_out[j, :, 128 * i:128 * (i + 1)] = factor
            approx = dot_n(basis, factor)
            err_out[:, cols] = corr[:, cols] - approx
            new_first = first_decay * first[:, cols] + (1.0 - first_decay) * approx
            new_second = second_decay * second[:, cols] + (1.0 - second_decay) * approx * approx
            first_out[:, cols] = new_first
            second_out[:, cols] = new_second
            first_hat = new_first / (1.0 - first_decay**step_count)
            second_hat = new_second / (1.0 - second_decay**step_count)
            w_out[:, cols] = weights[:, cols] - learn_rate * first_hat / (jnp.sqrt(second_hat) + adam_epsilon)


def local(activations, cotangents, error_buffer, master_weights, first_moment, second_moment, warm_factor):
    tokens = activations.shape[0]
    rows, cols = error_buffer.shape
    shape = jax.ShapeDtypeStruct
    vmem = pl.BlockSpec(memory_space=pltpu.VMEM)
    anywhere = pl.BlockSpec(memory_space=pltpu.HBM)
    copies = 120
    corr, pt, linv, n = pl.pallas_call(
        kernel_a,
        out_shape=(shape((rows, cols), F32), shape((128, 128), F32), shape((2, 64, 128), F32), shape((2, 256, 128), F32)),
        in_specs=[anywhere] * 4,
        out_specs=(vmem,) * 4,
        scratch_shapes=[
            pltpu.VMEM((4, 2 * tokens, 512), BF16),
            pltpu.VMEM((2, tokens, cols), BF16),
            pltpu.VMEM((cols, 2 * tokens), BF16),
            pltpu.VMEM((4, 4, cols, 128), F32),
            pltpu.VMEM((30, 528, 128), BF16),
            pltpu.VMEM((30, 528, 128), BF16),
            pltpu.VMEM((rows, cols), F32),
            pltpu.VMEM((2, 64, 512), F32),
            pltpu.VMEM((128, 128), F32),
            pltpu.VMEM((8, 16, 128), F32),
            pltpu.VMEM((16, 128), F32),
            pltpu.VMEM((2, 256, 128), F32),
            pltpu.VMEM((256, 128), F32),
            pltpu.VMEM((64, 128), F32),
            pltpu.VMEM((64, 128), F32),
            pltpu.VMEM((256, 128), F32),
            pltpu.VMEM((16, 16, 128), F32),
            pltpu.VMEM((16, 128), F32),
            pltpu.VMEM((8, 16, 128), F32),
            pltpu.VMEM((16, 128), F32),
            pltpu.VMEM((4, 32, 128), F32),
            pltpu.VMEM((4, 32, 128), F32),
            pltpu.VMEM((32, 128), F32),
            pltpu.VMEM((64, 128), F32),
            pltpu.VMEM((2, 64, 128), F32),
            pltpu.SemaphoreType.DMA((copies,)),
            pltpu.SemaphoreType.DMA((copies,)),
            pltpu.SemaphoreType.DMA((24,)),
        ],
        compiler_params=pltpu.CompilerParams(
            collective_id=0, has_side_effects=True, vmem_limit_bytes=60 * 1024 * 1024),
    )(activations, cotangents, error_buffer, warm_factor)
    tile = shape((rows, cols), F32)
    return pl.pallas_call(
        kernel_b,
        out_shape=(tile, tile, tile, tile, shape(warm_factor.shape, F32)),
        in_specs=[vmem] * 7,
        out_specs=(vmem,) * 5,
        compiler_params=pltpu.CompilerParams(vmem_limit_bytes=16 * 1024 * 1024),
    )(corr, pt, linv, n, master_weights, first_moment, second_moment)


def solution(mesh):
    placed = (
        P(("replica", "dp"), None),
        P(("replica", "dp"), None),
        P(("replica", "dp"), None),
        P("dp", None),
        P("dp", None),
        P("dp", None),
        P(),
    )
    return jax.shard_map(
        local,
        mesh=mesh,
        in_specs=placed,
        out_specs=(P("dp", None), P("dp", None), P("dp", None), P(("replica", "dp"), None), P()),
        check_vma=False,
    )
```

```python
import jax
import jax.numpy as jnp
from jax import lax
from jax.experimental import pallas as pl
from jax.experimental.pallas import tpu as pltpu
from jax.sharding import PartitionSpec as P

highest = lax.Precision.HIGHEST
first_decay = 0.9
second_decay = 0.999
learn_rate = 0.01
adam_epsilon = 1e-08
step_count = 10

F32 = jnp.float32
BF16 = jnp.bfloat16
DEPTH = 8
SPAN = 174.0
OFFSETS = (2, 1, 3, 0)


def dot_t(a, b):
    return lax.dot_general(a, b, (((1,), (1,)), ((), ())), precision=highest, preferred_element_type=F32)


def dot_n(a, b):
    return jnp.dot(a, b, precision=highest, preferred_element_type=F32)


def encode(source, code):
    tiles = [slice(128 * i, 128 * (i + 1)) for i in range(4)]
    top = jnp.abs(source[tiles[0], :])
    for tile in tiles[1:]:
        top = jnp.maximum(top, jnp.abs(source[tile, :]))
    top = jnp.maximum(jnp.max(top, axis=0, keepdims=True) * 1.004, 1e-30).astype(BF16)
    code[512:528, :] = jnp.broadcast_to(top, (16, 128))
    scale = SPAN / top.astype(F32)
    for tile in tiles:
        value = source[tile, :]
        size = jnp.exp(jnp.abs(value) * scale - 0.5 * SPAN)
        code[tile, :] = jnp.where(value < 0.0, -size, size).astype(BF16)


def decode(code, tile):
    scale = code[512:528, :].astype(F32)[0:1] * (1.0 / SPAN)
    value = code[tile, :].astype(F32)
    size = (jnp.log(jnp.abs(value)) + 0.5 * SPAN) * scale
    return jnp.where(value < 0.0, -size, size)


class Wire:
    def __init__(self, send, recv):
        self.send, self.recv, self.copies, self.drained = send, recv, [], 0

    def start(self, src, dst, device):
        i = len(self.copies)
        copy = pltpu.make_async_remote_copy(
            src_ref=src, dst_ref=dst, send_sem=self.send.at[i], recv_sem=self.recv.at[i],
            device_id=device, device_id_type=pl.DeviceIdType.MESH,
        )
        copy.start()
        self.copies.append(copy)
        return copy

    def drain(self):
        for copy in self.copies[self.drained:]:
            copy.wait_send()
        self.drained = len(self.copies)


class Local:
    def __init__(self, sems):
        self.sems, self.count = sems, 0

    def start(self, src, dst):
        copy = pltpu.make_async_copy(src, dst, self.sems.at[self.count])
        copy.start()
        self.count += 1
        return copy


def kernel_a(
    acts, cots, err, warm,
    corr_out, basis_out, linv_out, n_out,
    acts_v, cots_v, cots_t, own, tx, rx,
    err_v, warm_v, corr_v, pt_loc, zr, zsum, n_loc, n_rx, g_loc, g_rx, ns, ra, nb, zs, nz, ga, gb, g_half, g_all,
    t_mat, pt_v, basis_v, n_v, send_sem, recv_sem, loc_sem,
):
    z = lax.axis_index("replica")
    dp = lax.axis_index("dp")
    c = dp % 2
    x = dp // 8
    y = (dp // 2) % 4
    p = x * (1 - c) + y * c
    q = y * (1 - c) + x * c
    sa = 8 - 6 * c
    sb = 2 + 6 * c
    tokens = cots.shape[0]

    def at(pp, qq):
        return (z, (pp % 4) * sa + (qq % 4) * sb + c)

    def along_a(k):
        return at(p + k, q)

    def along_b(k):
        return at(p, q + k)

    def along_z(k):
        return ((z + k) % DEPTH, dp)

    partner = (z, dp + 1 - 2 * c)

    def own_cols(t, s):
        d = ((p + OFFSETS[s]) % 4) * sa + ((q + OFFSETS[t]) % 4) * sb + c
        return pl.ds(pl.multiple_of(d * 128, 128), 128)

    def partner_cols(t, s):
        d = ((q + OFFSETS[s]) % 4) * sb + ((p + OFFSETS[t]) % 4) * sa + 1 - c
        return pl.ds(pl.multiple_of(d * 128, 128), 128)

    wire = Wire(send_sem, recv_sem)
    local = Local(loc_sem)

    cots_here = local.start(cots, cots_v.at[0])
    acts_here = [[None] * 4 for _ in range(4)]
    acts_there = [[None] * 4 for _ in range(4)]
    for s in range(4):
        acts_here[0][s] = local.start(acts.at[:, own_cols(0, s)], acts_v.at[0, pl.ds(0, tokens), pl.ds(128 * s, 128)])

    barrier = pltpu.get_barrier_semaphore()
    friends = [partner] + [at(p + i, q + j) for i in range(4) for j in range(4) if i or j] + [along_z(k) for k in range(1, DEPTH)]
    for friend in friends:
        pl.semaphore_signal(barrier, inc=1, device_id=friend, device_id_type=pl.DeviceIdType.MESH)
    pl.semaphore_wait(barrier, len(friends))

    lo, hi = pl.ds(0, 512), pl.ds(512, 512)

    def swap_acts(t, s):
        acts_there[t][s] = wire.start(
            acts.at[:, partner_cols(t, s)], acts_v.at[t, pl.ds(tokens, tokens), pl.ds(128 * s, 128)], partner)

    swap_acts(0, 0)
    cots_there = [wire.start(cots.at[:, part], cots_v.at[1, :, part], partner) for part in (lo, hi)]
    for s in (1, 2, 3):
        swap_acts(0, s)
    for t in (1, 2, 3):
        for s in range(4):
            acts_here[t][s] = local.start(
                acts.at[:, own_cols(t, s)], acts_v.at[t, pl.ds(0, tokens), pl.ds(128 * s, 128)])
            swap_acts(t, s)
    err_copy = local.start(err, err_v)
    warm_copy = local.start(warm, warm_v)

    def turn(h, j):
        @pl.loop(4 * j, 4 * j + 4)
        def _(i):
            cols = pl.ds(pl.multiple_of(i * 128, 128), 128)
            cots_t[cols, h * tokens:(h + 1) * tokens] = cots_v[h, :, cols].T

    def product(t, first, last, j):
        @pl.loop(2 * j, 2 * j + 2)
        def _(i):
            rows = pl.ds(pl.multiple_of(i * 256, 256), 256)
            part = jnp.dot(cots_t[rows, :], acts_v[t, :, 128 * first:128 * last], preferred_element_type=F32)
            for s in range(first, last):
                own[t, s, rows, :] = part[:, 128 * (s - first):128 * (s - first + 1)]

    def arrive(t, *blocks):
        for s in blocks:
            acts_here[t][s].wait()
            acts_there[t][s].wait_recv()

    def compute(t):
        arrive(t, 0, 1, 2, 3)
        product(t, 0, 4, 0)
        product(t, 0, 4, 1)

    slots = []

    def ship(source, device):
        i = len(slots)
        encode(source, tx.at[i])
        slots.append(wire.start(tx.at[i], rx.at[i], device))
        return i

    def absorb(target, *arrived):
        for i in arrived:
            slots[i].wait_recv()
        for i in range(4):
            tile = slice(128 * i, 128 * (i + 1))
            total = target[tile, :]
            for slot in arrived:
                total = total + decode(rx.at[slot], tile)
            target[tile, :] = total

    relay_a, relay_b, outer_m, outer_p, inner_m, inner_p = ([None] * 4 for _ in range(6))

    def send_relay(t):
        relay_a[t] = ship(own.at[t, 0, lo], along_a(1))
        relay_b[t] = ship(own.at[t, 0, hi], along_a(3))

    def send_outer(t):
        outer_m[t] = ship(own.at[t, 1, hi], along_a(1))
        outer_p[t] = ship(own.at[t, 2, lo], along_a(3))

    def send_inner(t):
        absorb(own.at[t, 1, lo], relay_a[t])
        inner_m[t] = ship(own.at[t, 1, lo], along_a(1))
        absorb(own.at[t, 2, hi], relay_b[t])
        inner_p[t] = ship(own.at[t, 2, hi], along_a(3))

    def gather(t):
        absorb(own.at[t, 3, lo], outer_p[t], inner_m[t])
        absorb(own.at[t, 3, hi], outer_m[t], inner_p[t])

    cots_here.wait()
    turn(0, 0)
    turn(0, 1)
    arrive(0, 0)
    cots_there[0].wait_recv()
    turn(1, 0)
    product(0, 0, 1, 0)
    relay_a[0] = ship(own.at[0, 0, lo], along_a(1))
    cots_there[1].wait_recv()
    turn(1, 1)
    product(0, 0, 1, 1)
    relay_b[0] = ship(own.at[0, 0, hi], along_a(3))
    arrive(0, 1, 2)
    product(0, 1, 3, 1)
    outer_m[0] = ship(own.at[0, 1, hi], along_a(1))
    product(0, 1, 3, 0)
    outer_p[0] = ship(own.at[0, 2, lo], along_a(3))
    arrive(0, 3)
    product(0, 3, 4, 0)
    product(0, 3, 4, 1)
    compute(1)
    send_relay(1)
    send_inner(0)
    send_outer(1)
    compute(2)
    send_relay(2)
    send_inner(1)
    send_outer(2)
    gather(0)
    second_a = ship(own.at[0, 3, lo], along_b(1))
    second_b = ship(own.at[0, 3, hi], along_b(3))
    compute(3)
    send_relay(3)
    send_inner(2)
    send_outer(3)
    gather(1)
    outer2_m = ship(own.at[1, 3, hi], along_b(1))
    absorb(own.at[1, 3, lo], second_a)
    inner2_m = ship(own.at[1, 3, lo], along_b(1))
    send_inner(3)
    gather(2)
    outer2_p = ship(own.at[2, 3, lo], along_b(3))
    absorb(own.at[2, 3, hi], second_b)
    inner2_p = ship(own.at[2, 3, hi], along_b(3))

    err_copy.wait()
    for i in range(8):
        own[3, 3, 128 * i:128 * (i + 1), :] += err_v[:, 128 * i:128 * (i + 1)].T
    m_t = own.at[3, 3]
    absorb(own.at[3, 3, lo], outer_p[3], inner_m[3], outer2_p, inner2_m)
    absorb(own.at[3, 3, hi], outer_m[3], inner_p[3], outer2_m, inner2_p)

    warm_copy.wait()
    for j in range(2):
        pt_loc[64 * j:64 * (j + 1), :] = dot_n(warm_v[j], m_t[512 * j:512 * (j + 1), :])

    def z_rows(zz):
        return pl.ds(pl.multiple_of((zz % DEPTH) * 16, 16), 16)

    scatter = [wire.start(pt_loc.at[z_rows(z + k)], zr.at[k], along_z(k)) for k in range(1, DEPTH)]
    total = pt_loc[z_rows(z), :]
    for k in range(1, DEPTH):
        scatter[k - 1].wait_recv()
        total = total + zr[k]
    zsum[...] = total
    spread = [wire.start(zsum, pt_v.at[z_rows(z)], along_z(k)) for k in range(1, DEPTH)]
    pt_v[z_rows(z), :] = total
    for i in range(8):
        corr_v[:, 128 * i:128 * (i + 1)] = m_t[128 * i:128 * (i + 1), :].T
    corr_copy = local.start(corr_v, corr_out)
    wire.drain()
    for copy in spread:
        copy.wait_recv()

    pt = pt_v[...]
    lane = lax.broadcasted_iota(jnp.int32, (64, 128), 1)
    gram = dot_t(pt, pt)
    g_loc[...] = jnp.where(lane < 64, gram[0:64], gram[64:128])
    g_swap = wire.start(g_loc, g_rx, partner)
    for j in range(2):
        for i in range(4):
            n_loc[j, 64 * i:64 * (i + 1), :] = dot_t(
                pt[64 * j:64 * (j + 1)], m_t[512 * j + 128 * i:512 * j + 128 * (i + 1), :])
    n_swap = wire.start(n_loc.at[1 - c], n_rx, partner)

    half = pl.ds(pl.multiple_of(c * 32, 32), 32)
    g_swap.wait_recv()
    ga[p] = g_loc[half, :] + g_rx[half, :]
    ga_copies = [wire.start(ga.at[p], ga.at[p], along_a(k)) for k in (1, 2, 3)]

    n_swap.wait_recv()
    ns[...] = n_loc[c] + n_rx[...]

    def block(i, j):
        return pl.ds(pl.multiple_of((((p + i) % 4) * 4 + (q + j) % 4) * 16, 16), 16)

    others = [(i, j) for i in range(4) for j in range(4) if i or j]
    ra_copies = [wire.start(ns.at[block(i, j)], ra.at[4 * i + j], at(p + i, q + j)) for i, j in others]

    for copy in ga_copies:
        copy.wait_recv()
    gb[q] = (ga[0] + ga[1]) + (ga[2] + ga[3])
    gb_copies = [wire.start(gb.at[q], gb.at[q], along_b(k)) for k in (1, 2, 3)]

    for copy in ra_copies:
        copy.wait_recv()
    total = ns[block(0, 0), :]
    for i, j in others:
        total = total + ra[4 * i + j]
    nb[...] = total
    zs_copies = [wire.start(nb, zs.at[z], along_z(k)) for k in range(1, DEPTH)]
    zs[z] = nb[...]

    for copy in gb_copies:
        copy.wait_recv()
    g_part = (gb[0] + gb[1]) + (gb[2] + gb[3])
    g_half[...] = g_part
    g_all[half, :] = g_part
    g_back = wire.start(g_half, g_all.at[half], partner)

    g_back.wait_recv()
    row = lax.broadcasted_iota(jnp.int32, (64, 128), 0)
    g = g_all[...]
    eye = jnp.where(lane == row, 1.0, 0.0).astype(F32)
    t_mat[0] = jnp.where(lane >= 64, pltpu.roll(g, 64, 1), eye)
    t_mat[1] = jnp.where(lane >= 64, g, eye)
    row8 = lax.broadcasted_iota(jnp.int32, (8, 128), 0)

    def eliminate(first, last):
        low = first // 8
        mats = [[t_mat[j, 8 * i:8 * (i + 1), :] for i in range(low, 8)] for j in range(2)]
        for k in range(first, last, 2):
            top, sub = k // 8 - low, k % 8
            for mat in mats:
                left = [jnp.broadcast_to(part[:, 64 + k:65 + k], (8, 128)) for part in mat[top:]]
                right = [jnp.broadcast_to(part[:, 65 + k:66 + k], (8, 128)) for part in mat[top:]]
                one, two = mat[top][sub:sub + 1], mat[top][sub + 1:sub + 2]
                inv_one = 1.0 / left[0][sub:sub + 1]
                cross = right[0][sub:sub + 1]
                ratio = left[0][sub + 1:sub + 2] * inv_one
                two = two - ratio * one
                inv_two = 1.0 / (right[0][sub + 1:sub + 2] - ratio * cross)
                for i in range(len(left)):
                    by_one = left[i] * inv_one
                    by_two = (right[i] - by_one * cross) * inv_two
                    if i == 0:
                        by_one = jnp.where(row8 > sub, by_one, 0.0)
                        by_two = jnp.where(row8 > sub + 1, by_two, 0.0)
                    mat[top + i] = mat[top + i] - by_one * one - by_two * two
        for j in range(2):
            for i in range(low, 8):
                t_mat[j, 8 * i:8 * (i + 1), :] = mats[j][i - low]

    eliminate(0, 24)
    for copy in zs_copies:
        copy.wait_recv()
    nz[...] = ((zs[0] + zs[1]) + (zs[2] + zs[3])) + ((zs[4] + zs[5]) + (zs[6] + zs[7]))
    back = [wire.start(nz, n_v.at[c, block(0, 0)], at(p + i, q + j)) for i, j in others]
    n_v[c, block(0, 0), :] = nz[...]
    eliminate(24, 64)
    for copy in back:
        copy.wait_recv()
    back_c = wire.start(n_v.at[c], n_v.at[c], partner)
    n_copy = local.start(n_v.at[c], n_out.at[c])
    for j in range(2):
        for i in range(8):
            rows = slice(8 * i, 8 * (i + 1))
            part = t_mat[j, rows, :]
            diagonal = jnp.sum(jnp.where(lane[rows] == row[rows] + 64, part, 0.0), axis=1, keepdims=True)
            t_mat[j, rows, :] = part / jnp.sqrt(diagonal)
    linv_copy = local.start(t_mat, linv_out)
    for j in range(2):
        basis_v[64 * j:64 * (j + 1), :] = dot_n(t_mat[j, :, 0:64], pt[64 * j:64 * (j + 1)])
    basis_copy = local.start(basis_v, basis_out)
    back_c.wait_recv()
    n_rest = local.start(n_v.at[1 - c], n_out.at[1 - c])
    wire.drain()
    for copy in (corr_copy, n_copy, linv_copy, basis_copy, n_rest):
        copy.wait()


def kernel_b(
    corr, basis, linv, n, weights, first, second,
    w_out, first_out, second_out, err_out, factor_out,
    corr_v, basis_v, linv_v, n_v, weights_v, first_v, second_v, w_new, first_new, second_new, err_new, factor_new, sems,
):
    local = Local(sems)
    small = [local.start(a, b) for a, b in ((linv, linv_v), (n, n_v), (basis, basis_v))]
    large = [local.start(a, b) for a, b in ((corr, corr_v), (first, first_v), (second, second_v), (weights, weights_v))]
    for copy in small:
        copy.wait()
    bases = []
    stores = []
    for j in range(2):
        inverse = linv_v[j][:, 0:64]
        bases.append(basis_v[64 * j:64 * (j + 1), :].T)
        for i in range(4):
            factor_new[j, :, 128 * i:128 * (i + 1)] = dot_n(inverse, n_v[j, 64 * i:64 * (i + 1), :]) * 0.125
        stores.append(local.start(factor_new.at[j], factor_out.at[j]))
    for copy in large:
        copy.wait()
    for i in range(4):
        j, cols = i // 2, slice(256 * i, 256 * (i + 1))
        approx = dot_n(bases[j], factor_new[j, :, 256 * (i % 2):256 * (i % 2 + 1)])
        err_new[:, cols] = corr_v[:, cols] - approx
        new_first = first_decay * first_v[:, cols] + (1.0 - first_decay) * approx
        new_second = second_decay * second_v[:, cols] + (1.0 - second_decay) * approx * approx
        first_new[:, cols] = new_first
        second_new[:, cols] = new_second
        first_hat = new_first / (1.0 - first_decay**step_count)
        second_hat = new_second / (1.0 - second_decay**step_count)
        w_new[:, cols] = weights_v[:, cols] - learn_rate * first_hat / (jnp.sqrt(second_hat) + adam_epsilon)
        for a, b in ((err_new, err_out), (first_new, first_out), (second_new, second_out), (w_new, w_out)):
            stores.append(local.start(a.at[:, pl.ds(256 * i, 256)], b.at[:, pl.ds(256 * i, 256)]))
    for copy in stores:
        copy.wait()


def local(activations, cotangents, error_buffer, master_weights, first_moment, second_moment, warm_factor):
    tokens = activations.shape[0]
    rows, cols = error_buffer.shape
    shape = jax.ShapeDtypeStruct
    vmem = pl.BlockSpec(memory_space=pltpu.VMEM)
    anywhere = pl.BlockSpec(memory_space=pltpu.HBM)
    copies = 120
    corr, basis, linv, n = pl.pallas_call(
        kernel_a,
        out_shape=(shape((rows, cols), F32), shape((128, 128), F32), shape((2, 64, 128), F32), shape((2, 256, 128), F32)),
        in_specs=[anywhere] * 4,
        out_specs=(anywhere,) * 4,
        scratch_shapes=[
            pltpu.VMEM((4, 2 * tokens, 512), BF16),
            pltpu.VMEM((2, tokens, cols), BF16),
            pltpu.VMEM((cols, 2 * tokens), BF16),
            pltpu.VMEM((4, 4, cols, 128), F32),
            pltpu.VMEM((30, 528, 128), BF16),
            pltpu.VMEM((30, 528, 128), BF16),
            pltpu.VMEM((rows, cols), F32),
            pltpu.VMEM((2, 64, 512), F32),
            pltpu.VMEM((rows, cols), F32),
            pltpu.VMEM((128, 128), F32),
            pltpu.VMEM((8, 16, 128), F32),
            pltpu.VMEM((16, 128), F32),
            pltpu.VMEM((2, 256, 128), F32),
            pltpu.VMEM((256, 128), F32),
            pltpu.VMEM((64, 128), F32),
            pltpu.VMEM((64, 128), F32),
            pltpu.VMEM((256, 128), F32),
            pltpu.VMEM((16, 16, 128), F32),
            pltpu.VMEM((16, 128), F32),
            pltpu.VMEM((8, 16, 128), F32),
            pltpu.VMEM((16, 128), F32),
            pltpu.VMEM((4, 32, 128), F32),
            pltpu.VMEM((4, 32, 128), F32),
            pltpu.VMEM((32, 128), F32),
            pltpu.VMEM((64, 128), F32),
            pltpu.VMEM((2, 64, 128), F32),
            pltpu.VMEM((128, 128), F32),
            pltpu.VMEM((128, 128), F32),
            pltpu.VMEM((2, 256, 128), F32),
            pltpu.SemaphoreType.DMA((copies,)),
            pltpu.SemaphoreType.DMA((copies,)),
            pltpu.SemaphoreType.DMA((32,)),
        ],
        compiler_params=pltpu.CompilerParams(
            collective_id=0, has_side_effects=True, vmem_limit_bytes=60 * 1024 * 1024),
    )(activations, cotangents, error_buffer, warm_factor)
    tile = shape((rows, cols), F32)
    return pl.pallas_call(
        kernel_b,
        out_shape=(tile, tile, tile, tile, shape(warm_factor.shape, F32)),
        in_specs=[anywhere] * 7,
        out_specs=(anywhere,) * 5,
        scratch_shapes=[
            pltpu.VMEM((rows, cols), F32),
            pltpu.VMEM((128, 128), F32),
            pltpu.VMEM((2, 64, 128), F32),
            pltpu.VMEM((2, 256, 128), F32),
        ] + [pltpu.VMEM((rows, cols), F32)] * 7 + [
            pltpu.VMEM(warm_factor.shape, F32),
            pltpu.SemaphoreType.DMA((25,)),
        ],
        compiler_params=pltpu.CompilerParams(vmem_limit_bytes=60 * 1024 * 1024),
    )(corr, basis, linv, n, master_weights, first_moment, second_moment)


def solution(mesh):
    placed = (
        P(("replica", "dp"), None),
        P(("replica", "dp"), None),
        P(("replica", "dp"), None),
        P("dp", None),
        P("dp", None),
        P("dp", None),
        P(),
    )
    return jax.shard_map(
        local,
        mesh=mesh,
        in_specs=placed,
        out_specs=(P("dp", None), P("dp", None), P("dp", None), P(("replica", "dp"), None), P()),
        check_vma=False,
    )
```

```python
import jax
import jax.numpy as jnp
from jax import lax
from jax.experimental import pallas as pl
from jax.experimental.pallas import tpu as pltpu
from jax.sharding import PartitionSpec as P

highest = lax.Precision.HIGHEST
first_decay = 0.9
second_decay = 0.999
learn_rate = 0.01
adam_epsilon = 1e-08
step_count = 10

F32 = jnp.float32
BF16 = jnp.bfloat16
DEPTH = 8
SPAN = 174.0
OFFSETS = (2, 1, 3, 0)


def dot_t(a, b):
    return lax.dot_general(a, b, (((1,), (1,)), ((), ())), precision=highest, preferred_element_type=F32)


def dot_n(a, b):
    return jnp.dot(a, b, precision=highest, preferred_element_type=F32)


def encode(source, code):
    tiles = [slice(128 * i, 128 * (i + 1)) for i in range(4)]
    top = jnp.abs(source[tiles[0], :])
    for tile in tiles[1:]:
        top = jnp.maximum(top, jnp.abs(source[tile, :]))
    top = jnp.maximum(jnp.max(top, axis=0, keepdims=True) * 1.004, 1e-30).astype(BF16)
    code[512:528, :] = jnp.broadcast_to(top, (16, 128))
    scale = SPAN / top.astype(F32)
    for tile in tiles:
        value = source[tile, :]
        size = jnp.exp(jnp.abs(value) * scale - 0.5 * SPAN)
        code[tile, :] = jnp.where(value < 0.0, -size, size).astype(BF16)


def decode(code, tile):
    scale = code[512:528, :].astype(F32)[0:1] * (1.0 / SPAN)
    value = code[tile, :].astype(F32)
    size = (jnp.log(jnp.abs(value)) + 0.5 * SPAN) * scale
    return jnp.where(value < 0.0, -size, size)


class Wire:
    def __init__(self, send, recv):
        self.send, self.recv, self.copies, self.drained = send, recv, [], 0

    def start(self, src, dst, device):
        i = len(self.copies)
        copy = pltpu.make_async_remote_copy(
            src_ref=src, dst_ref=dst, send_sem=self.send.at[i], recv_sem=self.recv.at[i],
            device_id=device, device_id_type=pl.DeviceIdType.MESH,
        )
        copy.start()
        self.copies.append(copy)
        return copy

    def drain(self):
        for copy in self.copies[self.drained:]:
            copy.wait_send()
        self.drained = len(self.copies)


class Local:
    def __init__(self, sems):
        self.sems, self.count = sems, 0

    def start(self, src, dst):
        copy = pltpu.make_async_copy(src, dst, self.sems.at[self.count])
        copy.start()
        self.count += 1
        return copy


def kernel_a(
    acts, cots, err, warm,
    corr_out, basis_out, linv_out, n_out,
    acts_v, cots_v, cots_t, own, tx, rx,
    err_v, warm_v, corr_v, pt_loc, zr, zsum, n_loc, n_rx, g_loc, g_rx, ns, ra, nb, zs, nz, ga, gb, g_half, g_all,
    t_mat, pt_v, basis_v, n_v, send_sem, recv_sem, loc_sem, news_sem,
):
    z = lax.axis_index("replica")
    dp = lax.axis_index("dp")
    c = dp % 2
    x = dp // 8
    y = (dp // 2) % 4
    p = x * (1 - c) + y * c
    q = y * (1 - c) + x * c
    sa = 8 - 6 * c
    sb = 2 + 6 * c
    tokens = cots.shape[0]

    def at(pp, qq):
        return (z, (pp % 4) * sa + (qq % 4) * sb + c)

    def along_a(k):
        return at(p + k, q)

    def along_b(k):
        return at(p, q + k)

    def along_z(k):
        return ((z + k) % DEPTH, dp)

    partner = (z, dp + 1 - 2 * c)

    def own_cols(t, s):
        d = ((p + OFFSETS[s]) % 4) * sa + ((q + OFFSETS[t]) % 4) * sb + c
        return pl.ds(pl.multiple_of(d * 128, 128), 128)

    def partner_cols(t, s):
        d = ((q + OFFSETS[s]) % 4) * sb + ((p + OFFSETS[t]) % 4) * sa + 1 - c
        return pl.ds(pl.multiple_of(d * 128, 128), 128)

    wire = Wire(send_sem, recv_sem)
    local = Local(loc_sem)

    cots_here = local.start(cots, cots_v.at[0])
    acts_here = [[None] * 4 for _ in range(4)]
    acts_there = [[None] * 4 for _ in range(4)]
    for s in range(4):
        acts_here[0][s] = local.start(acts.at[:, own_cols(0, s)], acts_v.at[0, pl.ds(0, tokens), pl.ds(128 * s, 128)])

    barrier = pltpu.get_barrier_semaphore()
    friends = [partner, along_a(1), along_a(3), along_b(1), along_b(3), along_z(1), along_z(7)]
    for friend in friends:
        pl.semaphore_signal(barrier, inc=1, device_id=friend, device_id_type=pl.DeviceIdType.MESH)
    pl.semaphore_wait(barrier, len(friends))

    lo, hi = pl.ds(0, 512), pl.ds(512, 512)

    def swap_acts(t, s):
        acts_there[t][s] = wire.start(
            acts.at[:, partner_cols(t, s)], acts_v.at[t, pl.ds(tokens, tokens), pl.ds(128 * s, 128)], partner)

    swap_acts(0, 0)
    cots_there = [wire.start(cots.at[:, part], cots_v.at[1, :, part], partner) for part in (lo, hi)]
    for s in (1, 2, 3):
        swap_acts(0, s)
    for t in (1, 2, 3):
        for s in range(4):
            acts_here[t][s] = local.start(
                acts.at[:, own_cols(t, s)], acts_v.at[t, pl.ds(0, tokens), pl.ds(128 * s, 128)])
            swap_acts(t, s)
    err_copy = local.start(err, err_v)
    warm_copy = local.start(warm, warm_v)

    def tell(index, k):
        pl.semaphore_signal(
            news_sem.at[index], inc=1, device_id=along_z(k), device_id_type=pl.DeviceIdType.MESH)

    def hear(index):
        pl.semaphore_wait(news_sem.at[index], 1)

    def turn(h, j):
        @pl.loop(4 * j, 4 * j + 4)
        def _(i):
            cols = pl.ds(pl.multiple_of(i * 128, 128), 128)
            cots_t[cols, h * tokens:(h + 1) * tokens] = cots_v[h, :, cols].T

    def product(t, first, last, j):
        @pl.loop(2 * j, 2 * j + 2)
        def _(i):
            rows = pl.ds(pl.multiple_of(i * 256, 256), 256)
            part = jnp.dot(cots_t[rows, :], acts_v[t, :, 128 * first:128 * last], preferred_element_type=F32)
            for s in range(first, last):
                own[t, s, rows, :] = part[:, 128 * (s - first):128 * (s - first + 1)]

    def arrive(t, *blocks):
        for s in blocks:
            acts_here[t][s].wait()
            acts_there[t][s].wait_recv()

    def compute(t):
        arrive(t, 0, 1, 2, 3)
        product(t, 0, 4, 0)
        product(t, 0, 4, 1)

    slots = []

    def ship(source, device):
        i = len(slots)
        encode(source, tx.at[i])
        slots.append(wire.start(tx.at[i], rx.at[i], device))
        return i

    def absorb(target, *arrived):
        for i in arrived:
            slots[i].wait_recv()
        for i in range(4):
            tile = slice(128 * i, 128 * (i + 1))
            total = target[tile, :]
            for slot in arrived:
                total = total + decode(rx.at[slot], tile)
            target[tile, :] = total

    relay_a, relay_b, outer_m, outer_p, inner_m, inner_p = ([None] * 4 for _ in range(6))

    def send_relay(t):
        relay_a[t] = ship(own.at[t, 0, lo], along_a(1))
        relay_b[t] = ship(own.at[t, 0, hi], along_a(3))

    def send_outer(t):
        outer_m[t] = ship(own.at[t, 1, hi], along_a(1))
        outer_p[t] = ship(own.at[t, 2, lo], along_a(3))

    def send_inner(t):
        absorb(own.at[t, 1, lo], relay_a[t])
        inner_m[t] = ship(own.at[t, 1, lo], along_a(1))
        absorb(own.at[t, 2, hi], relay_b[t])
        inner_p[t] = ship(own.at[t, 2, hi], along_a(3))

    def gather(t):
        absorb(own.at[t, 3, lo], outer_p[t], inner_m[t])
        absorb(own.at[t, 3, hi], outer_m[t], inner_p[t])

    cots_here.wait()
    turn(0, 0)
    turn(0, 1)
    arrive(0, 0)
    cots_there[0].wait_recv()
    turn(1, 0)
    product(0, 0, 1, 0)
    relay_a[0] = ship(own.at[0, 0, lo], along_a(1))
    cots_there[1].wait_recv()
    turn(1, 1)
    product(0, 0, 1, 1)
    relay_b[0] = ship(own.at[0, 0, hi], along_a(3))
    arrive(0, 1, 2)
    product(0, 1, 3, 1)
    outer_m[0] = ship(own.at[0, 1, hi], along_a(1))
    product(0, 1, 3, 0)
    outer_p[0] = ship(own.at[0, 2, lo], along_a(3))
    arrive(0, 3)
    product(0, 3, 4, 0)
    product(0, 3, 4, 1)
    tell(0, 1)
    tell(1, 7)
    arrive(1, 0, 1, 2, 3)
    product(1, 0, 1, 0)
    product(1, 0, 1, 1)
    send_relay(1)
    send_inner(0)
    product(1, 1, 4, 0)
    product(1, 1, 4, 1)
    send_outer(1)
    hear(0)
    hear(1)
    tell(2, 1)
    tell(3, 7)
    arrive(2, 0, 1, 2, 3)
    product(2, 0, 1, 0)
    product(2, 0, 1, 1)
    send_relay(2)
    send_inner(1)
    product(2, 1, 4, 0)
    product(2, 1, 4, 1)
    send_outer(2)
    hear(2)
    hear(3)
    tell(4, 1)
    arrive(3, 0, 1, 2, 3)
    product(3, 0, 1, 0)
    product(3, 0, 1, 1)
    send_relay(3)
    gather(0)
    second_a = ship(own.at[0, 3, lo], along_b(1))
    second_b = ship(own.at[0, 3, hi], along_b(3))
    send_inner(2)
    product(3, 1, 4, 0)
    product(3, 1, 4, 1)
    send_outer(3)
    hear(4)
    gather(1)
    outer2_m = ship(own.at[1, 3, hi], along_b(1))
    absorb(own.at[1, 3, lo], second_a)
    inner2_m = ship(own.at[1, 3, lo], along_b(1))
    send_inner(3)
    gather(2)
    outer2_p = ship(own.at[2, 3, lo], along_b(3))
    absorb(own.at[2, 3, hi], second_b)
    inner2_p = ship(own.at[2, 3, hi], along_b(3))

    err_copy.wait()
    for i in range(8):
        own[3, 3, 128 * i:128 * (i + 1), :] += err_v[:, 128 * i:128 * (i + 1)].T
    m_t = own.at[3, 3]
    absorb(own.at[3, 3, lo], outer_p[3], inner_m[3], outer2_p, inner2_m)
    absorb(own.at[3, 3, hi], outer_m[3], inner_p[3], outer2_m, inner2_p)

    warm_copy.wait()
    for j in range(2):
        pt_loc[64 * j:64 * (j + 1), :] = dot_n(warm_v[j], m_t[512 * j:512 * (j + 1), :])

    def z_rows(zz):
        return pl.ds(pl.multiple_of((zz % DEPTH) * 16, 16), 16)

    scatter = [wire.start(pt_loc.at[z_rows(z + k)], zr.at[k], along_z(k)) for k in range(1, DEPTH)]
    total = pt_loc[z_rows(z), :]
    for k in range(1, DEPTH):
        scatter[k - 1].wait_recv()
        total = total + zr[k]
    zsum[...] = total
    spread = [wire.start(zsum, pt_v.at[z_rows(z)], along_z(k)) for k in range(1, DEPTH)]
    pt_v[z_rows(z), :] = total
    for i in range(8):
        corr_v[:, 128 * i:128 * (i + 1)] = m_t[128 * i:128 * (i + 1), :].T
    corr_copy = local.start(corr_v, corr_out)
    wire.drain()
    for copy in spread:
        copy.wait_recv()

    pt = pt_v[...]
    lane = lax.broadcasted_iota(jnp.int32, (64, 128), 1)
    gram = dot_t(pt, pt)
    g_loc[...] = jnp.where(lane < 64, gram[0:64], gram[64:128])
    g_swap = wire.start(g_loc, g_rx, partner)
    for j in range(2):
        part = dot_t(pt[64 * j:64 * (j + 1)], m_t[512 * j:512 * (j + 1), :])
        for i in range(4):
            n_loc[j, 64 * i:64 * (i + 1), :] = part[:, 128 * i:128 * (i + 1)]
    n_swap = wire.start(n_loc.at[1 - c], n_rx, partner)

    half = pl.ds(pl.multiple_of(c * 32, 32), 32)
    g_swap.wait_recv()
    ga[p] = g_loc[half, :] + g_rx[half, :]
    ga_copies = [wire.start(ga.at[p], ga.at[p], along_a(k)) for k in (1, 2, 3)]

    n_swap.wait_recv()
    ns[...] = n_loc[c] + n_rx[...]

    def block(i, j):
        return pl.ds(pl.multiple_of((((p + i) % 4) * 4 + (q + j) % 4) * 16, 16), 16)

    others = [(i, j) for i in range(4) for j in range(4) if i or j]
    ra_copies = [wire.start(ns.at[block(i, j)], ra.at[4 * i + j], at(p + i, q + j)) for i, j in others]

    for copy in ga_copies:
        copy.wait_recv()
    gb[q] = (ga[0] + ga[1]) + (ga[2] + ga[3])
    gb_copies = [wire.start(gb.at[q], gb.at[q], along_b(k)) for k in (1, 2, 3)]

    for copy in ra_copies:
        copy.wait_recv()
    total = ns[block(0, 0), :]
    for i, j in others:
        total = total + ra[4 * i + j]
    nb[...] = total
    zs_copies = [wire.start(nb, zs.at[z], along_z(k)) for k in range(1, DEPTH)]
    zs[z] = nb[...]

    for copy in gb_copies:
        copy.wait_recv()
    g_part = (gb[0] + gb[1]) + (gb[2] + gb[3])
    g_half[...] = g_part
    g_all[half, :] = g_part
    g_back = wire.start(g_half, g_all.at[half], partner)

    g_back.wait_recv()
    row = lax.broadcasted_iota(jnp.int32, (64, 128), 0)
    g = g_all[...]
    eye = jnp.where(lane == row, 1.0, 0.0).astype(F32)
    t_mat[0] = jnp.where(lane >= 64, pltpu.roll(g, 64, 1), eye)
    t_mat[1] = jnp.where(lane >= 64, g, eye)
    row8 = lax.broadcasted_iota(jnp.int32, (8, 128), 0)

    def eliminate(first, last):
        low = first // 8
        mats = [[t_mat[j, 8 * i:8 * (i + 1), :] for i in range(low, 8)] for j in range(2)]
        for k in range(first, last, 2):
            top, sub = k // 8 - low, k % 8
            for mat in mats:
                left = [jnp.broadcast_to(part[:, 64 + k:65 + k], (8, 128)) for part in mat[top:]]
                right = [jnp.broadcast_to(part[:, 65 + k:66 + k], (8, 128)) for part in mat[top:]]
                one, two = mat[top][sub:sub + 1], mat[top][sub + 1:sub + 2]
                inv_one = 1.0 / left[0][sub:sub + 1]
                cross = right[0][sub:sub + 1]
                ratio = left[0][sub + 1:sub + 2] * inv_one
                two = two - ratio * one
                inv_two = 1.0 / (right[0][sub + 1:sub + 2] - ratio * cross)
                for i in range(len(left)):
                    by_one = left[i] * inv_one
                    by_two = (right[i] - by_one * cross) * inv_two
                    if i == 0:
                        by_one = jnp.where(row8 > sub, by_one, 0.0)
                        by_two = jnp.where(row8 > sub + 1, by_two, 0.0)
                    mat[top + i] = mat[top + i] - by_one * one - by_two * two
        for j in range(2):
            for i in range(low, 8):
                t_mat[j, 8 * i:8 * (i + 1), :] = mats[j][i - low]

    eliminate(0, 24)
    for copy in zs_copies:
        copy.wait_recv()
    nz[...] = ((zs[0] + zs[1]) + (zs[2] + zs[3])) + ((zs[4] + zs[5]) + (zs[6] + zs[7]))
    back = [wire.start(nz, n_v.at[c, block(0, 0)], at(p + i, q + j)) for i, j in others]
    n_v[c, block(0, 0), :] = nz[...]
    eliminate(24, 64)
    for copy in back:
        copy.wait_recv()
    back_c = wire.start(n_v.at[c], n_v.at[c], partner)
    n_copy = local.start(n_v.at[c], n_out.at[c])
    for j in range(2):
        for i in range(8):
            rows = slice(8 * i, 8 * (i + 1))
            part = t_mat[j, rows, :]
            diagonal = jnp.sum(jnp.where(lane[rows] == row[rows] + 64, part, 0.0), axis=1, keepdims=True)
            t_mat[j, rows, :] = part / jnp.sqrt(diagonal)
    linv_copy = local.start(t_mat, linv_out)
    for j in range(2):
        basis_v[64 * j:64 * (j + 1), :] = dot_n(t_mat[j, :, 0:64], pt[64 * j:64 * (j + 1)])
    basis_copy = local.start(basis_v, basis_out)
    back_c.wait_recv()
    n_rest = local.start(n_v.at[1 - c], n_out.at[1 - c])
    wire.drain()
    for copy in (corr_copy, n_copy, linv_copy, basis_copy, n_rest):
        copy.wait()


def kernel_b(
    corr, basis, linv, n, weights, first, second,
    w_out, first_out, second_out, err_out, factor_out,
    corr_v, basis_v, linv_v, n_v, weights_v, first_v, second_v, w_new, first_new, second_new, err_new, factor_new, sems,
):
    local = Local(sems)
    small = [local.start(a, b) for a, b in ((linv, linv_v), (n, n_v), (basis, basis_v))]
    large = [local.start(a, b) for a, b in ((corr, corr_v), (first, first_v), (second, second_v), (weights, weights_v))]
    for copy in small:
        copy.wait()
    bases = []
    stores = []
    for j in range(2):
        inverse = linv_v[j][:, 0:64]
        bases.append(basis_v[64 * j:64 * (j + 1), :].T)
        total = jnp.concatenate([n_v[j, 64 * i:64 * (i + 1), :] for i in range(4)], axis=1)
        factor_new[j] = dot_n(inverse, total) * 0.125
        stores.append(local.start(factor_new.at[j], factor_out.at[j]))
    for copy in large:
        copy.wait()
    for i in range(4):
        j, cols = i // 2, slice(256 * i, 256 * (i + 1))
        approx = dot_n(bases[j], factor_new[j, :, 256 * (i % 2):256 * (i % 2 + 1)])
        err_new[:, cols] = corr_v[:, cols] - approx
        new_first = first_decay * first_v[:, cols] + (1.0 - first_decay) * approx
        new_second = second_decay * second_v[:, cols] + (1.0 - second_decay) * approx * approx
        first_new[:, cols] = new_first
        second_new[:, cols] = new_second
        first_hat = new_first / (1.0 - first_decay**step_count)
        second_hat = new_second / (1.0 - second_decay**step_count)
        w_new[:, cols] = weights_v[:, cols] - learn_rate * first_hat / (jnp.sqrt(second_hat) + adam_epsilon)
        for a, b in ((err_new, err_out), (first_new, first_out), (second_new, second_out), (w_new, w_out)):
            stores.append(local.start(a.at[:, pl.ds(256 * i, 256)], b.at[:, pl.ds(256 * i, 256)]))
    for copy in stores:
        copy.wait()


def local(activations, cotangents, error_buffer, master_weights, first_moment, second_moment, warm_factor):
    tokens = activations.shape[0]
    rows, cols = error_buffer.shape
    shape = jax.ShapeDtypeStruct
    vmem = pl.BlockSpec(memory_space=pltpu.VMEM)
    anywhere = pl.BlockSpec(memory_space=pltpu.HBM)
    copies = 120
    corr, basis, linv, n = pl.pallas_call(
        kernel_a,
        out_shape=(shape((rows, cols), F32), shape((128, 128), F32), shape((2, 64, 128), F32), shape((2, 256, 128), F32)),
        in_specs=[anywhere] * 4,
        out_specs=(anywhere,) * 4,
        scratch_shapes=[
            pltpu.VMEM((4, 2 * tokens, 512), BF16),
            pltpu.VMEM((2, tokens, cols), BF16),
            pltpu.VMEM((cols, 2 * tokens), BF16),
            pltpu.VMEM((4, 4, cols, 128), F32),
            pltpu.VMEM((30, 528, 128), BF16),
            pltpu.VMEM((30, 528, 128), BF16),
            pltpu.VMEM((rows, cols), F32),
            pltpu.VMEM((2, 64, 512), F32),
            pltpu.VMEM((rows, cols), F32),
            pltpu.VMEM((128, 128), F32),
            pltpu.VMEM((8, 16, 128), F32),
            pltpu.VMEM((16, 128), F32),
            pltpu.VMEM((2, 256, 128), F32),
            pltpu.VMEM((256, 128), F32),
            pltpu.VMEM((64, 128), F32),
            pltpu.VMEM((64, 128), F32),
            pltpu.VMEM((256, 128), F32),
            pltpu.VMEM((16, 16, 128), F32),
            pltpu.VMEM((16, 128), F32),
            pltpu.VMEM((8, 16, 128), F32),
            pltpu.VMEM((16, 128), F32),
            pltpu.VMEM((4, 32, 128), F32),
            pltpu.VMEM((4, 32, 128), F32),
            pltpu.VMEM((32, 128), F32),
            pltpu.VMEM((64, 128), F32),
            pltpu.VMEM((2, 64, 128), F32),
            pltpu.VMEM((128, 128), F32),
            pltpu.VMEM((128, 128), F32),
            pltpu.VMEM((2, 256, 128), F32),
            pltpu.SemaphoreType.DMA((copies,)),
            pltpu.SemaphoreType.DMA((copies,)),
            pltpu.SemaphoreType.DMA((32,)),
            pltpu.SemaphoreType.REGULAR((5,)),
        ],
        compiler_params=pltpu.CompilerParams(
            collective_id=0, has_side_effects=True, vmem_limit_bytes=60 * 1024 * 1024),
    )(activations, cotangents, error_buffer, warm_factor)
    tile = shape((rows, cols), F32)
    return pl.pallas_call(
        kernel_b,
        out_shape=(tile, tile, tile, tile, shape(warm_factor.shape, F32)),
        in_specs=[anywhere] * 7,
        out_specs=(anywhere,) * 5,
        scratch_shapes=[
            pltpu.VMEM((rows, cols), F32),
            pltpu.VMEM((128, 128), F32),
            pltpu.VMEM((2, 64, 128), F32),
            pltpu.VMEM((2, 256, 128), F32),
        ] + [pltpu.VMEM((rows, cols), F32)] * 7 + [
            pltpu.VMEM(warm_factor.shape, F32),
            pltpu.SemaphoreType.DMA((25,)),
        ],
        compiler_params=pltpu.CompilerParams(vmem_limit_bytes=60 * 1024 * 1024),
    )(corr, basis, linv, n, master_weights, first_moment, second_moment)


def solution(mesh):
    placed = (
        P(("replica", "dp"), None),
        P(("replica", "dp"), None),
        P(("replica", "dp"), None),
        P("dp", None),
        P("dp", None),
        P("dp", None),
        P(),
    )
    return jax.shard_map(
        local,
        mesh=mesh,
        in_specs=placed,
        out_specs=(P("dp", None), P("dp", None), P("dp", None), P(("replica", "dp"), None), P()),
        check_vma=False,
    )
```

```python
import jax
import jax.numpy as jnp
from jax import lax
from jax.experimental import pallas as pl
from jax.experimental.pallas import tpu as pltpu
from jax.sharding import PartitionSpec as P

highest = lax.Precision.HIGHEST
first_decay = 0.9
second_decay = 0.999
learn_rate = 0.01
adam_epsilon = 1e-08
step_count = 10

F32 = jnp.float32
BF16 = jnp.bfloat16
DEPTH = 8
SPAN = 174.0
OFFSETS = (2, 1, 3, 0)


def dot_t(a, b):
    return lax.dot_general(a, b, (((1,), (1,)), ((), ())), precision=highest, preferred_element_type=F32)


def dot_n(a, b):
    return jnp.dot(a, b, precision=highest, preferred_element_type=F32)


def encode(source, code):
    tiles = [slice(128 * i, 128 * (i + 1)) for i in range(4)]
    top = jnp.abs(source[tiles[0], :])
    for tile in tiles[1:]:
        top = jnp.maximum(top, jnp.abs(source[tile, :]))
    top = jnp.maximum(jnp.max(top, axis=0, keepdims=True) * 1.004, 1e-30).astype(BF16)
    code[512:528, :] = jnp.broadcast_to(top, (16, 128))
    scale = SPAN / top.astype(F32)
    for tile in tiles:
        value = source[tile, :]
        size = jnp.exp(jnp.abs(value) * scale - 0.5 * SPAN)
        code[tile, :] = jnp.where(value < 0.0, -size, size).astype(BF16)


def decode(code, tile):
    scale = code[512:528, :].astype(F32)[0:1] * (1.0 / SPAN)
    value = code[tile, :].astype(F32)
    size = (jnp.log(jnp.abs(value)) + 0.5 * SPAN) * scale
    return jnp.where(value < 0.0, -size, size)


class Wire:
    def __init__(self, send, recv):
        self.send, self.recv, self.copies, self.drained = send, recv, [], 0

    def start(self, src, dst, device):
        i = len(self.copies)
        copy = pltpu.make_async_remote_copy(
            src_ref=src, dst_ref=dst, send_sem=self.send.at[i], recv_sem=self.recv.at[i],
            device_id=device, device_id_type=pl.DeviceIdType.MESH,
        )
        copy.start()
        self.copies.append(copy)
        return copy

    def drain(self):
        for copy in self.copies[self.drained:]:
            copy.wait_send()
        self.drained = len(self.copies)


class Local:
    def __init__(self, sems):
        self.sems, self.count = sems, 0

    def start(self, src, dst):
        copy = pltpu.make_async_copy(src, dst, self.sems.at[self.count])
        copy.start()
        self.count += 1
        return copy


def kernel_a(
    acts, cots, err, warm,
    corr_out, basis_out, linv_out, n_out,
    acts_v, cots_v, cots_t, own, tx, rx,
    err_v, warm_v, corr_v, pt_loc, zr, zsum, n_loc, n_rx, g_loc, g_rx, ns, ra, nb, zs, nz, ga, gb, g_half, g_all,
    t_mat, pt_v, basis_v, n_v, send_sem, recv_sem, loc_sem, news_sem,
):
    z = lax.axis_index("replica")
    dp = lax.axis_index("dp")
    c = dp % 2
    x = dp // 8
    y = (dp // 2) % 4
    p = x * (1 - c) + y * c
    q = y * (1 - c) + x * c
    sa = 8 - 6 * c
    sb = 2 + 6 * c
    tokens = cots.shape[0]

    def at(pp, qq):
        return (z, (pp % 4) * sa + (qq % 4) * sb + c)

    def along_a(k):
        return at(p + k, q)

    def along_b(k):
        return at(p, q + k)

    def along_z(k):
        return ((z + k) % DEPTH, dp)

    partner = (z, dp + 1 - 2 * c)

    def own_cols(t, s):
        d = ((p + OFFSETS[s]) % 4) * sa + ((q + OFFSETS[t]) % 4) * sb + c
        return pl.ds(pl.multiple_of(d * 128, 128), 128)

    def partner_cols(t, s):
        d = ((q + OFFSETS[s]) % 4) * sb + ((p + OFFSETS[t]) % 4) * sa + 1 - c
        return pl.ds(pl.multiple_of(d * 128, 128), 128)

    wire = Wire(send_sem, recv_sem)
    local = Local(loc_sem)

    cots_here = local.start(cots, cots_v.at[0])
    acts_here = [[None] * 4 for _ in range(4)]
    acts_there = [[None] * 4 for _ in range(4)]
    for s in range(4):
        acts_here[0][s] = local.start(acts.at[:, own_cols(0, s)], acts_v.at[0, pl.ds(0, tokens), pl.ds(128 * s, 128)])

    barrier = pltpu.get_barrier_semaphore()
    friends = [partner, along_a(1), along_a(3), along_b(1), along_b(3), along_z(1), along_z(7)]
    for friend in friends:
        pl.semaphore_signal(barrier, inc=1, device_id=friend, device_id_type=pl.DeviceIdType.MESH)
    pl.semaphore_wait(barrier, len(friends))

    lo, hi = pl.ds(0, 512), pl.ds(512, 512)

    def swap_acts(t, s):
        acts_there[t][s] = wire.start(
            acts.at[:, partner_cols(t, s)], acts_v.at[t, pl.ds(tokens, tokens), pl.ds(128 * s, 128)], partner)

    swap_acts(0, 0)
    cots_there = [wire.start(cots.at[:, part], cots_v.at[1, :, part], partner) for part in (lo, hi)]
    for s in (1, 2, 3):
        swap_acts(0, s)
    for t in (1, 2, 3):
        for s in range(4):
            acts_here[t][s] = local.start(
                acts.at[:, own_cols(t, s)], acts_v.at[t, pl.ds(0, tokens), pl.ds(128 * s, 128)])
            swap_acts(t, s)
    err_copy = local.start(err, err_v)
    warm_copy = local.start(warm, warm_v)

    def tell(index, k):
        pl.semaphore_signal(
            news_sem.at[index], inc=1, device_id=along_z(k), device_id_type=pl.DeviceIdType.MESH)

    def hear(index):
        pl.semaphore_wait(news_sem.at[index], 1)

    def turn(h, j):
        @pl.loop(4 * j, 4 * j + 4)
        def _(i):
            cols = pl.ds(pl.multiple_of(i * 128, 128), 128)
            cots_t[cols, h * tokens:(h + 1) * tokens] = cots_v[h, :, cols].T

    def product(t, first, last, j):
        @pl.loop(2 * j, 2 * j + 2)
        def _(i):
            rows = pl.ds(pl.multiple_of(i * 256, 256), 256)
            part = jnp.dot(cots_t[rows, :], acts_v[t, :, 128 * first:128 * last], preferred_element_type=F32)
            for s in range(first, last):
                own[t, s, rows, :] = part[:, 128 * (s - first):128 * (s - first + 1)]

    def arrive(t, *blocks):
        for s in blocks:
            acts_here[t][s].wait()
            acts_there[t][s].wait_recv()

    def compute(t):
        arrive(t, 0, 1, 2, 3)
        product(t, 0, 4, 0)
        product(t, 0, 4, 1)

    slots = []

    def ship(source, device):
        i = len(slots)
        encode(source, tx.at[i])
        slots.append(wire.start(tx.at[i], rx.at[i], device))
        return i

    def absorb(target, *arrived):
        for i in arrived:
            slots[i].wait_recv()
        for i in range(4):
            tile = slice(128 * i, 128 * (i + 1))
            total = target[tile, :]
            for slot in arrived:
                total = total + decode(rx.at[slot], tile)
            target[tile, :] = total

    relay_a, relay_b, outer_m, outer_p, inner_m, inner_p = ([None] * 4 for _ in range(6))

    def send_relay(t):
        relay_a[t] = ship(own.at[t, 0, lo], along_a(1))
        relay_b[t] = ship(own.at[t, 0, hi], along_a(3))

    def send_outer(t):
        outer_m[t] = ship(own.at[t, 1, hi], along_a(1))
        outer_p[t] = ship(own.at[t, 2, lo], along_a(3))

    def send_inner(t):
        absorb(own.at[t, 1, lo], relay_a[t])
        inner_m[t] = ship(own.at[t, 1, lo], along_a(1))
        absorb(own.at[t, 2, hi], relay_b[t])
        inner_p[t] = ship(own.at[t, 2, hi], along_a(3))

    def gather(t):
        absorb(own.at[t, 3, lo], outer_p[t], inner_m[t])
        absorb(own.at[t, 3, hi], outer_m[t], inner_p[t])

    cots_here.wait()
    turn(0, 0)
    turn(0, 1)
    arrive(0, 0)
    cots_there[0].wait_recv()
    turn(1, 0)
    product(0, 0, 1, 0)
    relay_a[0] = ship(own.at[0, 0, lo], along_a(1))
    cots_there[1].wait_recv()
    turn(1, 1)
    product(0, 0, 1, 1)
    relay_b[0] = ship(own.at[0, 0, hi], along_a(3))
    arrive(0, 1, 2)
    product(0, 1, 3, 1)
    outer_m[0] = ship(own.at[0, 1, hi], along_a(1))
    product(0, 1, 3, 0)
    outer_p[0] = ship(own.at[0, 2, lo], along_a(3))
    arrive(0, 3)
    product(0, 3, 4, 0)
    product(0, 3, 4, 1)
    tell(0, 1)
    tell(1, 7)
    arrive(1, 0, 1, 2, 3)
    product(1, 0, 1, 0)
    product(1, 0, 1, 1)
    send_relay(1)
    send_inner(0)
    product(1, 1, 4, 0)
    product(1, 1, 4, 1)
    send_outer(1)
    hear(0)
    hear(1)
    tell(2, 1)
    tell(3, 7)
    arrive(2, 0, 1, 2, 3)
    product(2, 0, 1, 0)
    product(2, 0, 1, 1)
    send_relay(2)
    send_inner(1)
    product(2, 1, 4, 0)
    product(2, 1, 4, 1)
    send_outer(2)
    hear(2)
    hear(3)
    tell(4, 1)
    arrive(3, 0, 1, 2, 3)
    product(3, 0, 1, 0)
    product(3, 0, 1, 1)
    send_relay(3)
    gather(0)
    second_a = ship(own.at[0, 3, lo], along_b(1))
    second_b = ship(own.at[0, 3, hi], along_b(3))
    send_inner(2)
    product(3, 1, 4, 0)
    product(3, 1, 4, 1)
    send_outer(3)
    hear(4)
    gather(1)
    outer2_m = ship(own.at[1, 3, hi], along_b(1))
    absorb(own.at[1, 3, lo], second_a)
    inner2_m = ship(own.at[1, 3, lo], along_b(1))
    send_inner(3)
    gather(2)
    outer2_p = ship(own.at[2, 3, lo], along_b(3))
    absorb(own.at[2, 3, hi], second_b)
    inner2_p = ship(own.at[2, 3, hi], along_b(3))

    err_copy.wait()
    for i in range(8):
        own[3, 3, 128 * i:128 * (i + 1), :] += err_v[:, 128 * i:128 * (i + 1)].T
    m_t = own.at[3, 3]
    absorb(own.at[3, 3, lo], outer_p[3], inner2_m)
    absorb(own.at[3, 3, hi], outer_m[3], outer2_m)
    warm_copy.wait()
    absorb(own.at[3, 3, lo], inner_m[3], outer2_p)
    pt_loc[0:64, :] = dot_n(warm_v[0], m_t[0:512, :])
    absorb(own.at[3, 3, hi], inner_p[3], inner2_p)
    pt_loc[64:128, :] = dot_n(warm_v[1], m_t[512:1024, :])

    def z_rows(zz):
        return pl.ds(pl.multiple_of((zz % DEPTH) * 16, 16), 16)

    scatter = [wire.start(pt_loc.at[z_rows(z + k)], zr.at[k], along_z(k)) for k in range(1, DEPTH)]
    total = pt_loc[z_rows(z), :]
    for k in range(1, DEPTH):
        scatter[k - 1].wait_recv()
        total = total + zr[k]
    zsum[...] = total
    spread = [wire.start(zsum, pt_v.at[z_rows(z)], along_z(k)) for k in range(1, DEPTH)]
    pt_v[z_rows(z), :] = total
    for i in range(8):
        corr_v[:, 128 * i:128 * (i + 1)] = m_t[128 * i:128 * (i + 1), :].T
    corr_copy = local.start(corr_v, corr_out)
    wire.drain()
    for copy in spread:
        copy.wait_recv()

    pt = pt_v[...]
    lane = lax.broadcasted_iota(jnp.int32, (64, 128), 1)
    gram = dot_t(pt, pt)
    g_loc[...] = jnp.where(lane < 64, gram[0:64], gram[64:128])
    g_swap = wire.start(g_loc, g_rx, partner)
    for j in range(2):
        part = dot_t(pt[64 * j:64 * (j + 1)], m_t[512 * j:512 * (j + 1), :])
        for i in range(4):
            n_loc[j, 64 * i:64 * (i + 1), :] = part[:, 128 * i:128 * (i + 1)]
    n_swap = wire.start(n_loc.at[1 - c], n_rx, partner)

    half = pl.ds(pl.multiple_of(c * 32, 32), 32)
    g_swap.wait_recv()
    ga[p] = g_loc[half, :] + g_rx[half, :]
    ga_copies = [wire.start(ga.at[p], ga.at[p], along_a(k)) for k in (1, 2, 3)]

    n_swap.wait_recv()
    ns[...] = n_loc[c] + n_rx[...]

    def block(i, j):
        return pl.ds(pl.multiple_of((((p + i) % 4) * 4 + (q + j) % 4) * 16, 16), 16)

    others = [(i, j) for i in range(4) for j in range(4) if i or j]
    ra_copies = [wire.start(ns.at[block(i, j)], ra.at[4 * i + j], at(p + i, q + j)) for i, j in others]

    for copy in ga_copies:
        copy.wait_recv()
    gb[q] = (ga[0] + ga[1]) + (ga[2] + ga[3])
    gb_copies = [wire.start(gb.at[q], gb.at[q], along_b(k)) for k in (1, 2, 3)]

    for copy in ra_copies:
        copy.wait_recv()
    total = ns[block(0, 0), :]
    for i, j in others:
        total = total + ra[4 * i + j]
    nb[...] = total
    zs_copies = [wire.start(nb, zs.at[z], along_z(k)) for k in range(1, DEPTH)]
    zs[z] = nb[...]

    for copy in gb_copies:
        copy.wait_recv()
    g_part = (gb[0] + gb[1]) + (gb[2] + gb[3])
    g_half[...] = g_part
    g_all[half, :] = g_part
    g_back = wire.start(g_half, g_all.at[half], partner)

    g_back.wait_recv()
    row = lax.broadcasted_iota(jnp.int32, (64, 128), 0)
    g = g_all[...]
    eye = jnp.where(lane == row, 1.0, 0.0).astype(F32)
    t_mat[0] = jnp.where(lane >= 64, pltpu.roll(g, 64, 1), eye)
    t_mat[1] = jnp.where(lane >= 64, g, eye)
    row8 = lax.broadcasted_iota(jnp.int32, (8, 128), 0)

    def eliminate(first, last):
        low = first // 8
        mats = [[t_mat[j, 8 * i:8 * (i + 1), :] for i in range(low, 8)] for j in range(2)]
        for k in range(first, last, 2):
            top, sub = k // 8 - low, k % 8
            for mat in mats:
                left = [jnp.broadcast_to(part[:, 64 + k:65 + k], (8, 128)) for part in mat[top:]]
                right = [jnp.broadcast_to(part[:, 65 + k:66 + k], (8, 128)) for part in mat[top:]]
                one, two = mat[top][sub:sub + 1], mat[top][sub + 1:sub + 2]
                inv_one = 1.0 / left[0][sub:sub + 1]
                cross = right[0][sub:sub + 1]
                ratio = left[0][sub + 1:sub + 2] * inv_one
                two = two - ratio * one
                inv_two = 1.0 / (right[0][sub + 1:sub + 2] - ratio * cross)
                for i in range(len(left)):
                    by_one = left[i] * inv_one
                    by_two = (right[i] - by_one * cross) * inv_two
                    if i == 0:
                        by_one = jnp.where(row8 > sub, by_one, 0.0)
                        by_two = jnp.where(row8 > sub + 1, by_two, 0.0)
                    mat[top + i] = mat[top + i] - by_one * one - by_two * two
        for j in range(2):
            for i in range(low, 8):
                t_mat[j, 8 * i:8 * (i + 1), :] = mats[j][i - low]

    eliminate(0, 24)
    for copy in zs_copies:
        copy.wait_recv()
    nz[...] = ((zs[0] + zs[1]) + (zs[2] + zs[3])) + ((zs[4] + zs[5]) + (zs[6] + zs[7]))
    back = [wire.start(nz, n_v.at[c, block(0, 0)], at(p + i, q + j)) for i, j in others]
    n_v[c, block(0, 0), :] = nz[...]
    eliminate(24, 64)
    for copy in back:
        copy.wait_recv()
    back_c = wire.start(n_v.at[c], n_v.at[c], partner)
    n_copy = local.start(n_v.at[c], n_out.at[c])
    for j in range(2):
        for i in range(8):
            rows = slice(8 * i, 8 * (i + 1))
            part = t_mat[j, rows, :]
            diagonal = jnp.sum(jnp.where(lane[rows] == row[rows] + 64, part, 0.0), axis=1, keepdims=True)
            t_mat[j, rows, :] = part / jnp.sqrt(diagonal)
    linv_copy = local.start(t_mat, linv_out)
    for j in range(2):
        basis_v[64 * j:64 * (j + 1), :] = dot_n(t_mat[j, :, 0:64], pt[64 * j:64 * (j + 1)])
    basis_copy = local.start(basis_v, basis_out)
    back_c.wait_recv()
    n_rest = local.start(n_v.at[1 - c], n_out.at[1 - c])
    wire.drain()
    for copy in (corr_copy, n_copy, linv_copy, basis_copy, n_rest):
        copy.wait()


def kernel_b(
    corr, basis, linv, n, weights, first, second,
    w_out, first_out, second_out, err_out, factor_out,
    corr_v, basis_v, linv_v, n_v, weights_v, first_v, second_v, w_new, first_new, second_new, err_new, factor_new, sems,
):
    local = Local(sems)
    small = [local.start(a, b) for a, b in ((linv, linv_v), (n, n_v), (basis, basis_v))]
    large = [local.start(a, b) for a, b in ((corr, corr_v), (first, first_v), (second, second_v), (weights, weights_v))]
    for copy in small:
        copy.wait()
    stores = []
    for i in range(4):
        j, cols = i // 2, slice(256 * i, 256 * (i + 1))
        if i % 2 == 0:
            total = jnp.concatenate([n_v[j, 64 * k:64 * (k + 1), :] for k in range(4)], axis=1)
            factor_new[j] = dot_n(linv_v[j][:, 0:64], total) * 0.125
            basis_t = basis_v[64 * j:64 * (j + 1), :].T
            stores.append(local.start(factor_new.at[j], factor_out.at[j]))
        approx = dot_n(basis_t, factor_new[j, :, 256 * (i % 2):256 * (i % 2 + 1)])
        if i == 0:
            for copy in large:
                copy.wait()
        err_new[:, cols] = corr_v[:, cols] - approx
        new_first = first_decay * first_v[:, cols] + (1.0 - first_decay) * approx
        new_second = second_decay * second_v[:, cols] + (1.0 - second_decay) * approx * approx
        first_new[:, cols] = new_first
        second_new[:, cols] = new_second
        first_hat = new_first * (learn_rate / (1.0 - first_decay**step_count))
        second_hat = new_second * (1.0 / (1.0 - second_decay**step_count))
        w_new[:, cols] = weights_v[:, cols] - first_hat / (jnp.sqrt(second_hat) + adam_epsilon)
        for a, b in ((err_new, err_out), (first_new, first_out), (second_new, second_out), (w_new, w_out)):
            stores.append(local.start(a.at[:, pl.ds(256 * i, 256)], b.at[:, pl.ds(256 * i, 256)]))
    for copy in stores:
        copy.wait()


def local(activations, cotangents, error_buffer, master_weights, first_moment, second_moment, warm_factor):
    tokens = activations.shape[0]
    rows, cols = error_buffer.shape
    shape = jax.ShapeDtypeStruct
    vmem = pl.BlockSpec(memory_space=pltpu.VMEM)
    anywhere = pl.BlockSpec(memory_space=pltpu.HBM)
    copies = 120
    corr, basis, linv, n = pl.pallas_call(
        kernel_a,
        out_shape=(shape((rows, cols), F32), shape((128, 128), F32), shape((2, 64, 128), F32), shape((2, 256, 128), F32)),
        in_specs=[anywhere] * 4,
        out_specs=(anywhere,) * 4,
        scratch_shapes=[
            pltpu.VMEM((4, 2 * tokens, 512), BF16),
            pltpu.VMEM((2, tokens, cols), BF16),
            pltpu.VMEM((cols, 2 * tokens), BF16),
            pltpu.VMEM((4, 4, cols, 128), F32),
            pltpu.VMEM((30, 528, 128), BF16),
            pltpu.VMEM((30, 528, 128), BF16),
            pltpu.VMEM((rows, cols), F32),
            pltpu.VMEM((2, 64, 512), F32),
            pltpu.VMEM((rows, cols), F32),
            pltpu.VMEM((128, 128), F32),
            pltpu.VMEM((8, 16, 128), F32),
            pltpu.VMEM((16, 128), F32),
            pltpu.VMEM((2, 256, 128), F32),
            pltpu.VMEM((256, 128), F32),
            pltpu.VMEM((64, 128), F32),
            pltpu.VMEM((64, 128), F32),
            pltpu.VMEM((256, 128), F32),
            pltpu.VMEM((16, 16, 128), F32),
            pltpu.VMEM((16, 128), F32),
            pltpu.VMEM((8, 16, 128), F32),
            pltpu.VMEM((16, 128), F32),
            pltpu.VMEM((4, 32, 128), F32),
            pltpu.VMEM((4, 32, 128), F32),
            pltpu.VMEM((32, 128), F32),
            pltpu.VMEM((64, 128), F32),
            pltpu.VMEM((2, 64, 128), F32),
            pltpu.VMEM((128, 128), F32),
            pltpu.VMEM((128, 128), F32),
            pltpu.VMEM((2, 256, 128), F32),
            pltpu.SemaphoreType.DMA((copies,)),
            pltpu.SemaphoreType.DMA((copies,)),
            pltpu.SemaphoreType.DMA((32,)),
            pltpu.SemaphoreType.REGULAR((5,)),
        ],
        compiler_params=pltpu.CompilerParams(
            collective_id=0, has_side_effects=True, vmem_limit_bytes=60 * 1024 * 1024),
    )(activations, cotangents, error_buffer, warm_factor)
    tile = shape((rows, cols), F32)
    return pl.pallas_call(
        kernel_b,
        out_shape=(tile, tile, tile, tile, shape(warm_factor.shape, F32)),
        in_specs=[anywhere] * 7,
        out_specs=(anywhere,) * 5,
        scratch_shapes=[
            pltpu.VMEM((rows, cols), F32),
            pltpu.VMEM((128, 128), F32),
            pltpu.VMEM((2, 64, 128), F32),
            pltpu.VMEM((2, 256, 128), F32),
        ] + [pltpu.VMEM((rows, cols), F32)] * 7 + [
            pltpu.VMEM(warm_factor.shape, F32),
            pltpu.SemaphoreType.DMA((25,)),
        ],
        compiler_params=pltpu.CompilerParams(vmem_limit_bytes=60 * 1024 * 1024),
    )(corr, basis, linv, n, master_weights, first_moment, second_moment)


def solution(mesh):
    placed = (
        P(("replica", "dp"), None),
        P(("replica", "dp"), None),
        P(("replica", "dp"), None),
        P("dp", None),
        P("dp", None),
        P("dp", None),
        P(),
    )
    return jax.shard_map(
        local,
        mesh=mesh,
        in_specs=placed,
        out_specs=(P("dp", None), P("dp", None), P("dp", None), P(("replica", "dp"), None), P()),
        check_vma=False,
    )
```
